512 devices in a mesh: tr: 8 (over y), tc: 4 (over z_lo), ga: 16 (over x, z_hi, core).
Axes of the slice: x: 4, y: 8, z: 8 (z_hi: 2, z_lo: 4; z = z_hi * 4 + z_lo), core: 2. Of those that a mesh axis runs over, the one named last changes fastest.
Arguments:
- valence: bfloat16 [2, 16, 64, 4096], P(None, None, 'ga'), may hold values from -6 to 6
- conduction: bfloat16 [2, 16, 64, 4096], P(None, None, 'ga'), may hold values from -6 to 6
- envelope: bfloat16 [2, 64, 4096], P(None, 'ga'), may hold values from -6 to 6
- valence_index: int32 [256], P(('tr', 'tc')), may hold values from 0 to 15, as said below
- conduction_index: int32 [256], P(('tr', 'tc')), may hold values from 0 to 15, as said below
- grid_index: int32 [10240], replicated, may hold values from 0 to 262143, as said below
- coulomb: float32 [10240], P('ga'), may hold values from 0.1 to 10
Outputs:
- kernel_panel: float32 [2, 256, 256], P(None, ('tr', 'tc'), 'ga')
The draws below stay inside these ranges and needn't reach their ends.
Inputs may be any that keep to these rules, and one draw needn't show every extreme that they name: `grid_index`: entries are distinct; block k of 640 entries (entries k * 640 to (k + 1) * 640 - 1) has ky in k * 4 to (k + 1) * 4 - 1. `valence_index`: valence_index[t] * 16 + conduction_index[t] takes each value of 0 to 255 once, so every pair of a valence band and a conduction band stands at exactly one transition. `conduction_index`: together with valence_index, every pair of a valence band and a conduction band stands at exactly one transition.
All inputs are finite; a program needn't handle non-finite values.
Results may differ from the reference program's by a relative error of at most 0.0005.
Values may be sent and summed in bfloat16 or wider, within the bound.
No kernel may reach another device: no remote copies, remote signals or barrier semaphores. Data moves between devices by JAX's collectives and lax.ppermute only.
A program may use at most 192 MiB of HBM per device.

```python
import math
import jax
import jax.numpy as jnp
from jax import lax

N = 64
NV = 16
G_DEV = 640
SLAB = 4
TRANS = 256
NC = 16
NG = 10240
N_GA = 16


def transition_pairs(key):
    return jax.random.permutation(key, TRANS).astype(jnp.int32)


def draw_valence_index(key, part):
    pairs = transition_pairs(key)
    return (pairs // NC).astype(jnp.int32)


def draw_conduction_index(key, part):
    pairs = transition_pairs(key)
    return (pairs % NC).astype(jnp.int32)


def draw_grid_index(key, part):
    key = jax.random.fold_in(key, 7)
    points = SLAB * N * N

    def one_block(block):
        block_key = jax.random.fold_in(key, block)
        first_key, second_key = jax.random.split(block_key)
        chosen = jax.random.permutation(first_key, points - 2)[:G_DEV - 2].astype(jnp.int32) + 1
        local = jnp.concatenate([jnp.array([0, points - 1], jnp.int32), chosen])
        local = jax.random.permutation(second_key, local)
        wave_x = local // (SLAB * N)
        remainder = local % (SLAB * N)
        return wave_x * N * N + block * SLAB * N + remainder
    return jax.vmap(one_block)(jnp.arange(N_GA, dtype=jnp.int32)).reshape(-1).astype(jnp.int32)


def block_levels(key, shape, cuts, low, largest):
    def one(axis_at, parts):
        steps = jax.random.uniform(jax.random.fold_in(jax.random.fold_in(key, 6), axis_at), (parts,), jnp.float32, low / len(cuts), largest / len(cuts))
        return jnp.repeat(jnp.exp(steps), shape[axis_at] // parts).reshape((-1,) + (1,) * (len(shape) - axis_at - 1))

    gain = one(*cuts[0])
    for cut in cuts[1:]:
        gain = gain * one(*cut)
    return gain


def gaussian(own_key, shape, spread, most, cuts=(), kind=jnp.bfloat16):
    values = jax.random.normal(own_key, shape, jnp.float32) * spread
    if len(cuts) > 0:
        values = block_levels(own_key, shape, cuts, -0.22, 0.18) * values
    return jnp.clip(values, min=-most, max=most).astype(kind)


def setup_inputs(seed: int = 0) -> dict:
    streams_of = jax.random.split(jax.random.key(seed), 8)
    valence = gaussian(streams_of[0], (2, NV, N, N * N), 1.0, 6.0, ((2, 16),))
    conduction = gaussian(streams_of[1], (2, NC, N, N * N), 1.0, 6.0, ((2, 16),))
    envelope = gaussian(streams_of[2], (2, N, N * N), 1.0, 6.0, ((1, 16),))
    valence_index = draw_valence_index(jax.random.fold_in(streams_of[7], 71), 0)
    conduction_index = draw_conduction_index(jax.random.fold_in(streams_of[7], 71), 0)
    grid_index = draw_grid_index(jax.random.fold_in(streams_of[7], 71), 0)
    coulomb = jnp.clip(jnp.exp(math.log(10.0) - 4.6051702 * jax.random.uniform(streams_of[6], (NG,), jnp.float32) ** block_levels(streams_of[6], (NG,), ((0, 16),), -0.2, 0.2)), 0.1, 10.0)
    return dict(valence=valence, conduction=conduction, envelope=envelope, valence_index=valence_index, conduction_index=conduction_index, grid_index=grid_index, coulomb=coulomb)


def reference(valence, conduction, envelope, valence_index, conduction_index, grid_index, coulomb):
    block_size = 16
    count = TRANS // block_size
    weight_root = jnp.sqrt(coulomb)
    valence_grid = valence.reshape(2, NV, N, N, N)
    conduct_grid = conduction.reshape(2, NC, N, N, N)
    common = envelope.reshape(2, N, N, N).astype(jnp.float32)

    def one_block(number):
        start = number * block_size
        valence_ids = lax.dynamic_slice_in_dim(valence_index, start, block_size)
        conduct_ids = lax.dynamic_slice_in_dim(conduction_index, start, block_size)
        valence_rows = jnp.take(valence_grid, valence_ids, axis=1).astype(jnp.float32)
        conduct_rows = jnp.take(conduct_grid, conduct_ids, axis=1).astype(jnp.float32) + common[:, None]
        real_part = valence_rows[0] * conduct_rows[0] + valence_rows[1] * conduct_rows[1]
        imag_part = valence_rows[0] * conduct_rows[1] - valence_rows[1] * conduct_rows[0]
        spectral = jnp.fft.fftn(real_part + 1j * imag_part, axes=(1, 2, 3), norm='ortho')
        spectral = spectral.reshape(block_size, N * N * N)
        picked = jnp.take(spectral, grid_index, axis=1)
        real_out = (jnp.real(picked) * weight_root).astype(jnp.bfloat16)
        imag_out = (jnp.imag(picked) * weight_root).astype(jnp.bfloat16)
        return jnp.stack([real_out, imag_out])
    blocks = lax.map(one_block, jnp.arange(count, dtype=jnp.int32))
    weighted = jnp.transpose(blocks, (1, 0, 2, 3)).reshape(2, TRANS, NG)
    real_w = weighted[0]
    imag_w = weighted[1]
    kernel_real = jnp.dot(real_w, real_w.T, preferred_element_type=jnp.float32) + jnp.dot(imag_w, imag_w.T, preferred_element_type=jnp.float32)
    kernel_imag = jnp.dot(real_w, imag_w.T, preferred_element_type=jnp.float32) - jnp.dot(imag_w, real_w.T, preferred_element_type=jnp.float32)
    return jnp.stack([kernel_real, kernel_imag]) * (1.0 / NG)
```

```python
import functools
import math

import jax
import jax.numpy as jnp
import numpy as np
from jax import lax
from jax.experimental import pallas as pl
from jax.experimental.pallas import tpu as pltpu
from jax.sharding import PartitionSpec as P

LANES = 128
COUNT = 8
SLAB = 4


def halves(array):
    high = array.astype(jnp.bfloat16)
    low = (array - high.astype(jnp.float32)).astype(jnp.bfloat16)
    return high, low


def tables(points):
    indices = np.arange(points)
    angles = 2.0 * np.pi * (np.outer(indices, indices) % points) / points
    pair = np.eye(2)
    along_z = np.concatenate([np.kron(pair, np.cos(angles)), np.kron(pair, np.sin(angles))], axis=1)
    half = points // 2
    short = np.arange(half)
    angles = 2.0 * np.pi * (np.outer(short, short) % half) / half
    planes = np.eye(SLAB)
    cosine, sine = np.kron(np.cos(angles), planes), np.kron(np.sin(angles), planes)
    along_y = np.block([[cosine, sine], [-sine, cosine]])
    turn = 2.0 * np.pi * np.repeat(short, SLAB) / points
    ones = np.ones((half * SLAB, points))
    twist = np.stack(
        [
            np.concatenate([ones, ones * np.cos(turn)[:, None]], axis=1),
            np.concatenate([0.0 * ones, ones * -np.sin(turn)[:, None]], axis=1),
        ]
    )

    return tuple(table.astype(np.float32) for table in (along_z, along_y, twist))


def unit_circle(steps, points):
    quarter = points // 4
    shifted = steps + quarter // 2
    turn = (shifted // quarter) & 3
    angle = ((shifted & (quarter - 1)) - quarter // 2).astype(jnp.float32) * (2.0 * math.pi / points)
    square = angle * angle
    sine = angle * (
        1.0 + square * (-1 / 6 + square * (1 / 120 + square * (-1 / 5040 + square * (1 / 362880))))
    )
    cosine = 1.0 + square * (
        -1 / 2
        + square * (1 / 24 + square * (-1 / 720 + square * (1 / 40320 - square * (1 / 3628800))))
    )
    odd = (turn & 1) == 1
    first = jnp.where(odd, sine, cosine)
    second = jnp.where(odd, cosine, sine)
    return (
        jnp.where((turn == 1) | (turn == 2), -first, first),
        jnp.where(turn >= 2, -second, second),
    )


def transform_kernel(
    points,
    valence_ids,
    conduct_ids,
    position,
    valence,
    conduction,
    envelope,
    grid,
    along_z,
    along_y,
    twist,
    out,
    field,
    waves,
):
    rows = points // 2 * SLAB
    tiles = grid.shape[0] // out.shape[0]
    blocks = out.shape[0]
    dot = functools.partial(jnp.dot, preferred_element_type=jnp.float32)

    wave_x = grid[...] // (points * points)
    for plane in range(SLAB):
        steps = ((position[0] * SLAB + plane) * wave_x) & (points - 1)
        cosine, sine = unit_circle(steps, points)
        waves[2 * plane] = cosine
        waves[2 * plane + 1] = sine

    z_high, z_low = halves(along_z[...])
    y_high, y_low = halves(along_y[...])

    common_real = envelope[0].astype(jnp.float32)
    common_imag = envelope[1].astype(jnp.float32)
    lane = lax.broadcasted_iota(jnp.int32, (rows, LANES), 1)
    sign = jnp.where(lane < points, 1.0, -1.0).astype(jnp.float32)
    for first in range(0, COUNT, 2):
        parts = []
        for t in (first, first + 1):
            v, c = valence_ids[t], conduct_ids[t]
            left_real = valence[0, v].astype(jnp.float32)
            left_imag = valence[1, v].astype(jnp.float32)
            right_real = conduction[0, c].astype(jnp.float32) + common_real
            right_imag = conduction[1, c].astype(jnp.float32) + common_imag
            parts.append(left_real * right_real + left_imag * right_imag)
            parts.append(left_real * right_imag - left_imag * right_real)
        high, low = halves(jnp.concatenate(parts, axis=0))
        moved = dot(high, z_high) + (dot(low, z_high) + dot(high, z_low))
        columns = []
        for t in range(2):
            real = moved[2 * t * rows : (2 * t + 1) * rows]
            imag = moved[(2 * t + 1) * rows : (2 * t + 2) * rows]
            columns.append(
                jnp.concatenate(
                    [real[:, :LANES] + imag[:, LANES:], imag[:, :LANES] - real[:, LANES:]], axis=0
                )
            )
        high, low = halves(jnp.concatenate(columns, axis=1))
        moved = dot(y_high, high) + (dot(y_high, low) + dot(y_low, high))
        for t in range(2):
            real = moved[:rows, t * LANES : (t + 1) * LANES]
            imag = moved[rows:, t * LANES : (t + 1) * LANES]
            turned_real = real * twist[0] - imag * twist[1]
            turned_imag = real * twist[1] + imag * twist[0]
            start = (first + t) * rows
            field[0, start : start + rows] = pltpu.roll(turned_real, points, 1) + sign * turned_real
            field[1, start : start + rows] = pltpu.roll(turned_imag, points, 1) + sign * turned_imag

    half = blocks // 2

    def one_pair(k, carry):
        picked = []
        for part in range(2):
            for y in range(SLAB):
                for x in range(SLAB):
                    start = (k * SLAB + y) * SLAB + x
                    picked.append(field[part, pl.ds(start, COUNT, stride=rows), :])
        high, low = halves(jnp.concatenate(picked, axis=0))
        source = jnp.concatenate([high, low], axis=1)
        chosen = []
        for side in range(2):
            row = (k + half * side) * tiles
            index = [grid[pl.ds(row + j, 1), :] for j in range(tiles)]
            depth = lax.broadcasted_iota(jnp.int32, (points, LANES), 0)
            match = jnp.concatenate(
                [jnp.where((i & (points - 1)) == depth, 1.0, 0.0) for i in index], axis=1
            ).astype(jnp.bfloat16)
            empty = jnp.zeros_like(match)
            order = [match, empty] if side == 0 else [empty, match]
            chosen.append(jnp.concatenate(order + order, axis=0))
        values = dot(source, jnp.concatenate(chosen, axis=1))
        for side in range(2):
            block = k + half * side
            for j in range(tiles):
                row = block * tiles + j
                at = (side * tiles + j) * LANES
                index = jnp.broadcast_to(grid[pl.ds(row, 1), :], (COUNT, LANES))
                wave_y = (index // points) & (SLAB - 1)
                total_real = jnp.zeros((COUNT, LANES), jnp.float32)
                total_imag = jnp.zeros((COUNT, LANES), jnp.float32)
                for x in range(SLAB):
                    pieces = []
                    for part in range(2):
                        of = [
                            values[((part * SLAB + y) * SLAB + x) * COUNT :][:COUNT, at : at + LANES]
                            for y in range(SLAB)
                        ]
                        pieces.append(
                            jnp.where(
                                wave_y < 2,
                                jnp.where(wave_y == 0, of[0], of[1]),
                                jnp.where(wave_y == 2, of[2], of[3]),
                            )
                        )
                    cosine = waves[2 * x, pl.ds(row, 1), :]
                    sine = waves[2 * x + 1, pl.ds(row, 1), :]
                    total_real += pieces[0] * cosine + pieces[1] * sine
                    total_imag += pieces[1] * cosine - pieces[0] * sine
                out[block, j * 2 * COUNT : (j * 2 + 1) * COUNT] = total_real.astype(out.dtype)
                out[block, (j * 2 + 1) * COUNT : (j * 2 + 2) * COUNT] = total_imag.astype(out.dtype)
        return carry

    lax.fori_loop(0, half, one_pair, 0)


def weight_kernel(scale, partial, coulomb, out):
    total = partial[0].astype(jnp.float32)
    for source in range(1, partial.shape[0]):
        total += partial[source].astype(jnp.float32)
    root = jnp.sqrt(coulomb[...])
    height = 2 * COUNT
    pieces = []
    for j in range(total.shape[0] // height):
        factor = root[:, j * LANES : (j + 1) * LANES]
        pieces.append((total[j * height : (j + 1) * height] * scale) * factor)
    weighted = jnp.concatenate(pieces, axis=0).astype(jnp.bfloat16)
    for target in range(out.shape[0]):
        out[target] = weighted


def panel_kernel(own, gathered, out):
    senders, height = gathered.shape[0], 2 * COUNT
    tiles = gathered.shape[1] // height
    first, second, right = [], [], []
    for j in range(tiles):
        left = own[0, j * height : (j + 1) * height].astype(jnp.float32)
        real, imag = left[:COUNT], left[COUNT:]
        empty = jnp.zeros((LANES - height, LANES), jnp.float32)
        first.append(jnp.concatenate([real, -imag, empty], axis=0).astype(jnp.bfloat16))
        second.append(jnp.concatenate([imag, real, empty], axis=0).astype(jnp.bfloat16))
        right.append(gathered[:, j * height : (j + 1) * height].reshape(senders * height, LANES))
    right = jnp.concatenate(right, axis=1)
    contract = (((1,), (1,)), ((), ()))

    def product(left):
        result = lax.dot_general(
            right, jnp.concatenate(left, axis=1), contract, preferred_element_type=jnp.float32
        )
        return result.reshape(senders, 2, COUNT, LANES)

    total = product(first)[:, 0] + product(second)[:, 1]
    out[...] = total.reshape(out.shape)


def sum_kernel(scale, partial, out):
    total = partial[0]
    for source in range(1, partial.shape[0]):
        total += partial[source]
    turned = (total * scale).T[: 2 * COUNT]
    out[...] = turned[:, : out.shape[2]].reshape(out.shape)


def body(valence, conduction, envelope, valence_index, conduction_index, grid_index, coulomb):
    points = math.isqrt(valence.shape[-1])
    groups = lax.axis_size("ga")
    senders = lax.axis_size("tr") * lax.axis_size("tc")
    per_device = coulomb.shape[0]
    tiles = per_device // LANES
    rows = points // 2 * SLAB
    transitions = senders * COUNT

    def turned(array):
        lead = array.shape[:-2]
        split = array.reshape(lead + (SLAB, points // 2, LANES))
        return jnp.swapaxes(split, -3, -2).reshape(lead + (rows, LANES))

    along_z, along_y, twist = tables(points)
    position = lax.axis_index("ga").astype(jnp.int32).reshape(1)
    smem = pl.BlockSpec(memory_space=pltpu.SMEM)
    vmem = pl.BlockSpec(memory_space=pltpu.VMEM)
    limit = pltpu.CompilerParams(vmem_limit_bytes=40 * 1024 * 1024)
    partial = pl.pallas_call(
        functools.partial(transform_kernel, points),
        out_shape=jax.ShapeDtypeStruct((groups, tiles * 2 * COUNT, LANES), jnp.float32),
        in_specs=[smem] * 3 + [vmem] * 7,
        out_specs=vmem,
        scratch_shapes=[
            pltpu.VMEM((2, COUNT * rows, LANES), jnp.float32),
            pltpu.VMEM((2 * SLAB, groups * tiles, LANES), jnp.float32),
        ],
        compiler_params=limit,
        name="transform",
    )(
        valence_index,
        conduction_index,
        position,
        turned(valence),
        turned(conduction),
        turned(envelope),
        grid_index.reshape(groups * tiles, LANES),
        along_z,
        along_y,
        twist,
    )
    partial = lax.all_to_all(partial, "ga", split_axis=0, concat_axis=0, tiled=True)
    copies = pl.pallas_call(
        functools.partial(weight_kernel, float(points) ** -1.5),
        out_shape=jax.ShapeDtypeStruct((senders, tiles * 2 * COUNT, LANES), jnp.bfloat16),
        in_specs=[vmem] * 2,
        out_specs=vmem,
        compiler_params=limit,
        name="weight",
    )(partial, coulomb.reshape(1, per_device))
    gathered = lax.all_to_all(copies, ("tr", "tc"), split_axis=0, concat_axis=0, tiled=True)
    width = transitions // groups
    terms = pl.pallas_call(
        panel_kernel,
        out_shape=jax.ShapeDtypeStruct((groups, width, LANES), jnp.float32),
        in_specs=[vmem] * 2,
        out_specs=vmem,
        compiler_params=limit,
        name="panel",
    )(copies, gathered)
    terms = lax.all_to_all(terms, "ga", split_axis=0, concat_axis=0, tiled=True)
    return pl.pallas_call(
        functools.partial(sum_kernel, 1.0 / (per_device * groups)),
        out_shape=jax.ShapeDtypeStruct((2, COUNT, width), jnp.float32),
        in_specs=[vmem],
        out_specs=vmem,
        compiler_params=limit,
        name="total",
    )(terms)


def solution(mesh):
    placed = (
        P(None, None, "ga", None),
        P(None, None, "ga", None),
        P(None, "ga", None),
        P(("tr", "tc")),
        P(("tr", "tc")),
        P(),
        P("ga"),
    )
    return jax.shard_map(
        body, mesh=mesh, in_specs=placed, out_specs=P(None, ("tr", "tc"), "ga"), check_vma=False
    )
```

```python
import functools
import math

import jax
import jax.numpy as jnp
import numpy as np
from jax import lax
from jax.experimental import pallas as pl
from jax.experimental.pallas import tpu as pltpu
from jax.sharding import PartitionSpec as P

LANES = 128
COUNT = 8
SLAB = 4


def halves(array):
    high = array.astype(jnp.bfloat16)
    low = (array - high.astype(jnp.float32)).astype(jnp.bfloat16)
    return high, low


def tables(points):
    indices = np.arange(points)
    angles = 2.0 * np.pi * (np.outer(indices, indices) % points) / points
    pair = np.eye(2)
    along_z = np.concatenate([np.kron(pair, np.cos(angles)), np.kron(pair, np.sin(angles))], axis=1)
    half = points // 2
    short = np.arange(half)
    angles = 2.0 * np.pi * (np.outer(short, short) % half) / half
    planes = np.eye(SLAB)
    cosine, sine = np.kron(np.cos(angles), planes), np.kron(np.sin(angles), planes)
    along_y = np.block([[cosine, sine], [-sine, cosine]])
    turn = 2.0 * np.pi * np.repeat(short, SLAB) / points
    ones = np.ones((half * SLAB, points))
    twist = np.stack(
        [
            np.concatenate([ones, ones * np.cos(turn)[:, None]], axis=1),
            np.concatenate([0.0 * ones, ones * -np.sin(turn)[:, None]], axis=1),
        ]
    )

    return tuple(table.astype(np.float32) for table in (along_z, along_y, twist))


def unit_circle(steps, points):
    quarter = points // 4
    shifted = steps + quarter // 2
    turn = (shifted // quarter) & 3
    angle = ((shifted & (quarter - 1)) - quarter // 2).astype(jnp.float32) * (2.0 * math.pi / points)
    square = angle * angle
    sine = angle * (
        1.0 + square * (-1 / 6 + square * (1 / 120 + square * (-1 / 5040 + square * (1 / 362880))))
    )
    cosine = 1.0 + square * (
        -1 / 2
        + square * (1 / 24 + square * (-1 / 720 + square * (1 / 40320 - square * (1 / 3628800))))
    )
    odd = (turn & 1) == 1
    first = jnp.where(odd, sine, cosine)
    second = jnp.where(odd, cosine, sine)
    return (
        jnp.where((turn == 1) | (turn == 2), -first, first),
        jnp.where(turn >= 2, -second, second),
    )


def transform_kernel(
    points,
    valence_ids,
    conduct_ids,
    position,
    valence,
    conduction,
    envelope,
    grid_source,
    along_z_source,
    along_y_source,
    twist_source,
    out,
    left_rows,
    right_rows,
    common,
    grid,
    along_z,
    along_y,
    twist,
    field,
    waves,
    arrived,
):
    rows = points // 2 * SLAB
    tiles = grid.shape[0] // out.shape[0]
    blocks = out.shape[0]
    dot = functools.partial(jnp.dot, preferred_element_type=jnp.float32)

    copies = []

    def fetch(source, target):
        copy = pltpu.make_async_copy(source, target, arrived.at[len(copies)])
        copy.start()
        copies.append(copy)
        return copy

    whole = [
        fetch(source, target)
        for source, target in (
            (grid_source, grid),
            (along_z_source, along_z),
            (envelope, common),
            (along_y_source, along_y),
            (twist_source, twist),
        )
    ]
    bands = []
    for t in range(COUNT):
        bands.append(
            (
                fetch(valence.at[:, valence_ids[t]], left_rows.at[t]),
                fetch(conduction.at[:, conduct_ids[t]], right_rows.at[t]),
            )
        )
    whole[0].wait()

    wave_x = grid[...] // (points * points)
    for plane in range(SLAB):
        steps = ((position[0] * SLAB + plane) * wave_x) & (points - 1)
        cosine, sine = unit_circle(steps, points)
        waves[2 * plane] = cosine
        waves[2 * plane + 1] = sine

    for copy in whole[1:]:
        copy.wait()
    z_high, z_low = halves(along_z[...])
    y_high, y_low = halves(along_y[...])

    common_real = common[0].astype(jnp.float32)
    common_imag = common[1].astype(jnp.float32)
    lane = lax.broadcasted_iota(jnp.int32, (rows, LANES), 1)
    sign = jnp.where(lane < points, 1.0, -1.0).astype(jnp.float32)
    for first in range(0, COUNT, 2):
        parts = []
        for t in (first, first + 1):
            for copy in bands[t]:
                copy.wait()
            left_real = left_rows[t, 0].astype(jnp.float32)
            left_imag = left_rows[t, 1].astype(jnp.float32)
            right_real = right_rows[t, 0].astype(jnp.float32) + common_real
            right_imag = right_rows[t, 1].astype(jnp.float32) + common_imag
            parts.append(left_real * right_real + left_imag * right_imag)
            parts.append(left_real * right_imag - left_imag * right_real)
        high, low = halves(jnp.concatenate(parts, axis=0))
        moved = dot(high, z_high) + (dot(low, z_high) + dot(high, z_low))
        columns = []
        for t in range(2):
            real = moved[2 * t * rows : (2 * t + 1) * rows]
            imag = moved[(2 * t + 1) * rows : (2 * t + 2) * rows]
            columns.append(
                jnp.concatenate(
                    [real[:, :LANES] + imag[:, LANES:], imag[:, :LANES] - real[:, LANES:]], axis=0
                )
            )
        high, low = halves(jnp.concatenate(columns, axis=1))
        moved = dot(y_high, high) + (dot(y_high, low) + dot(y_low, high))
        for t in range(2):
            real = moved[:rows, t * LANES : (t + 1) * LANES]
            imag = moved[rows:, t * LANES : (t + 1) * LANES]
            turned_real = real * twist[0] - imag * twist[1]
            turned_imag = real * twist[1] + imag * twist[0]
            start = (first + t) * rows
            field[0, start : start + rows] = pltpu.roll(turned_real, points, 1) + sign * turned_real
            field[1, start : start + rows] = pltpu.roll(turned_imag, points, 1) + sign * turned_imag

    half = blocks // 2

    def one_pair(k, carry):
        picked = []
        for part in range(2):
            for y in range(SLAB):
                for x in range(SLAB):
                    start = (k * SLAB + y) * SLAB + x
                    picked.append(field[part, pl.ds(start, COUNT, stride=rows), :])
        high, low = halves(jnp.concatenate(picked, axis=0))
        source = jnp.concatenate([high, low], axis=1)
        chosen = []
        for side in range(2):
            row = (k + half * side) * tiles
            index = [grid[pl.ds(row + j, 1), :] for j in range(tiles)]
            depth = lax.broadcasted_iota(jnp.int32, (points, LANES), 0)
            match = jnp.concatenate(
                [jnp.where((i & (points - 1)) == depth, 1.0, 0.0) for i in index], axis=1
            ).astype(jnp.bfloat16)
            empty = jnp.zeros_like(match)
            order = [match, empty] if side == 0 else [empty, match]
            chosen.append(jnp.concatenate(order + order, axis=0))
        values = dot(source, jnp.concatenate(chosen, axis=1))
        for side in range(2):
            block = k + half * side
            for j in range(tiles):
                row = block * tiles + j
                at = (side * tiles + j) * LANES
                index = jnp.broadcast_to(grid[pl.ds(row, 1), :], (COUNT, LANES))
                wave_y = (index // points) & (SLAB - 1)
                total_real = jnp.zeros((COUNT, LANES), jnp.float32)
                total_imag = jnp.zeros((COUNT, LANES), jnp.float32)
                for x in range(SLAB):
                    pieces = []
                    for part in range(2):
                        of = [
                            values[((part * SLAB + y) * SLAB + x) * COUNT :][:COUNT, at : at + LANES]
                            for y in range(SLAB)
                        ]
                        pieces.append(
                            jnp.where(
                                wave_y < 2,
                                jnp.where(wave_y == 0, of[0], of[1]),
                                jnp.where(wave_y == 2, of[2], of[3]),
                            )
                        )
                    cosine = waves[2 * x, pl.ds(row, 1), :]
                    sine = waves[2 * x + 1, pl.ds(row, 1), :]
                    total_real += pieces[0] * cosine + pieces[1] * sine
                    total_imag += pieces[1] * cosine - pieces[0] * sine
                out[block, j * 2 * COUNT : (j * 2 + 1) * COUNT] = total_real.astype(out.dtype)
                out[block, (j * 2 + 1) * COUNT : (j * 2 + 2) * COUNT] = total_imag.astype(out.dtype)
        return carry

    lax.fori_loop(0, half, one_pair, 0)


def weight_kernel(scale, partial, coulomb, out):
    total = partial[0].astype(jnp.float32)
    for source in range(1, partial.shape[0]):
        total += partial[source].astype(jnp.float32)
    root = jnp.sqrt(coulomb[...])
    height = 2 * COUNT
    pieces = []
    for j in range(total.shape[0] // height):
        factor = root[:, j * LANES : (j + 1) * LANES]
        pieces.append((total[j * height : (j + 1) * height] * scale) * factor)
    out[...] = jnp.concatenate(pieces, axis=0).astype(jnp.bfloat16)


def stack_kernel(position, *refs):
    pieces, out = refs[:-1], refs[-1]
    for shift, piece in enumerate(pieces):
        out[(position[0] - shift + len(pieces)) % len(pieces)] = piece[...]


def panel_kernel(place, own, *refs):
    tcs = place[1]
    chips = lax.axis_size("tc")
    stacks, outs, (gathered, terms) = refs[:chips], refs[chips:-2], refs[-2:]
    lines = stacks[0].shape[0]
    for shift, stack in enumerate(stacks):
        line = (tcs - shift + chips) % chips
        for other in range(lines):
            gathered[other * chips + line] = stack[other]
    senders, height = lines * chips, 2 * COUNT
    tiles = gathered.shape[1] // height
    first, second, right = [], [], []
    for j in range(tiles):
        left = own[j * height : (j + 1) * height].astype(jnp.float32)
        real, imag = left[:COUNT], left[COUNT:]
        empty = jnp.zeros((LANES - height, LANES), jnp.float32)
        first.append(jnp.concatenate([real, -imag, empty], axis=0).astype(jnp.bfloat16))
        second.append(jnp.concatenate([imag, real, empty], axis=0).astype(jnp.bfloat16))
        right.append(gathered[:, j * height : (j + 1) * height].reshape(senders * height, LANES))
    right = jnp.concatenate(right, axis=1)
    contract = (((1,), (1,)), ((), ()))

    def product(left):
        result = lax.dot_general(
            right, jnp.concatenate(left, axis=1), contract, preferred_element_type=jnp.float32
        )
        return result.reshape(senders, 2, COUNT, LANES)

    total = product(first)[:, 0] + product(second)[:, 1]
    terms[...] = total.reshape(terms.shape)
    for partner, out in enumerate(outs):
        out[...] = terms[place[0] ^ partner]


def sum_kernel(scale, *refs):
    out = refs[-1]
    total = refs[0][...]
    for piece in refs[1:-1]:
        total += piece[...]
    turned = (total * scale).T[: 2 * COUNT]
    out[...] = turned[:, : out.shape[2]].reshape(out.shape)


def body(valence, conduction, envelope, valence_index, conduction_index, grid_index, coulomb):
    points = math.isqrt(valence.shape[-1])
    groups, lines, chips = (lax.axis_size(name) for name in ("ga", "tr", "tc"))
    per_device = coulomb.shape[0]
    tiles = per_device // LANES
    rows = points // 2 * SLAB
    height = tiles * 2 * COUNT
    width = lines * chips * COUNT // groups

    def turned(array):
        lead = array.shape[:-2]
        split = array.reshape(lead + (SLAB, points // 2, LANES))
        return jnp.swapaxes(split, -3, -2).reshape(lead + (rows, LANES))

    position, line, chip = (
        lax.axis_index(name).astype(jnp.int32).reshape(1) for name in ("ga", "tr", "tc")
    )
    smem = pl.BlockSpec(memory_space=pltpu.SMEM)
    vmem = pl.BlockSpec(memory_space=pltpu.VMEM)
    anywhere = pl.BlockSpec(memory_space=pl.ANY)
    limit = pltpu.CompilerParams(vmem_limit_bytes=16 * 1024 * 1024)
    along_z, along_y, twist = tables(points)
    partial = pl.pallas_call(
        functools.partial(transform_kernel, points),
        out_shape=jax.ShapeDtypeStruct((groups, height, LANES), jnp.float32),
        in_specs=[smem] * 3 + [anywhere] * 7,
        out_specs=vmem,
        scratch_shapes=[
            pltpu.VMEM((COUNT, 2, rows, LANES), jnp.bfloat16),
            pltpu.VMEM((COUNT, 2, rows, LANES), jnp.bfloat16),
            pltpu.VMEM((2, rows, LANES), jnp.bfloat16),
            pltpu.VMEM((groups * tiles, LANES), jnp.int32),
            pltpu.VMEM(along_z.shape, jnp.float32),
            pltpu.VMEM(along_y.shape, jnp.float32),
            pltpu.VMEM(twist.shape, jnp.float32),
            pltpu.VMEM((2, COUNT * rows, LANES), jnp.float32),
            pltpu.VMEM((2 * SLAB, groups * tiles, LANES), jnp.float32),
            pltpu.SemaphoreType.DMA((5 + 2 * COUNT,)),
        ],
        compiler_params=pltpu.CompilerParams(vmem_limit_bytes=62 * 1024 * 1024),
        name="transform",
    )(
        valence_index,
        conduction_index,
        position,
        turned(valence),
        turned(conduction),
        turned(envelope),
        grid_index.reshape(groups * tiles, LANES),
        along_z,
        along_y,
        twist,
    )
    partial = lax.all_to_all(partial, "ga", split_axis=0, concat_axis=0, tiled=True)
    own = pl.pallas_call(
        functools.partial(weight_kernel, float(points) ** -1.5),
        out_shape=jax.ShapeDtypeStruct((height, LANES), jnp.bfloat16),
        in_specs=[vmem] * 2,
        out_specs=vmem,
        compiler_params=limit,
        name="weight",
    )(partial, coulomb.reshape(1, per_device))

    def shifted(array, name, shift):
        size = lax.axis_size(name)
        return lax.ppermute(array, name, [(i, (i + shift) % size) for i in range(size)])

    pieces = [own] + [shifted(own, "tr", shift) for shift in range(1, lines)]
    stack = pl.pallas_call(
        stack_kernel,
        out_shape=jax.ShapeDtypeStruct((lines, height, LANES), jnp.bfloat16),
        in_specs=[smem] + [vmem] * lines,
        out_specs=vmem,
        compiler_params=limit,
        name="stack",
    )(line, *pieces)
    stacks = [stack] + [shifted(stack, "tc", shift) for shift in range(1, chips)]
    terms = pl.pallas_call(
        panel_kernel,
        out_shape=[jax.ShapeDtypeStruct((width, LANES), jnp.float32)] * groups,
        in_specs=[smem] + [vmem] * (1 + chips),
        out_specs=[vmem] * groups,
        scratch_shapes=[
            pltpu.VMEM((lines * chips, height, LANES), jnp.bfloat16),
            pltpu.VMEM((groups, width, LANES), jnp.float32),
        ],
        compiler_params=limit,
        name="panel",
    )(jnp.concatenate([position, chip]), own, *stacks)
    pieces = [terms[0]] + [
        lax.ppermute(terms[partner], "ga", [(i, i ^ partner) for i in range(groups)])
        for partner in range(1, groups)
    ]
    return pl.pallas_call(
        functools.partial(sum_kernel, 1.0 / (per_device * groups)),
        out_shape=jax.ShapeDtypeStruct((2, COUNT, width), jnp.float32),
        in_specs=[vmem] * groups,
        out_specs=vmem,
        compiler_params=limit,
        name="total",
    )(*pieces)


def solution(mesh):
    placed = (
        P(None, None, "ga", None),
        P(None, None, "ga", None),
        P(None, "ga", None),
        P(("tr", "tc")),
        P(("tr", "tc")),
        P(),
        P("ga"),
    )
    return jax.shard_map(
        body, mesh=mesh, in_specs=placed, out_specs=P(None, ("tr", "tc"), "ga"), check_vma=False
    )
```

```python
import functools
import math

import jax
import jax.numpy as jnp
import numpy as np
from jax import lax
from jax.experimental import pallas as pl
from jax.experimental.pallas import tpu as pltpu
from jax.sharding import PartitionSpec as P

LANES = 128
COUNT = 8
SLAB = 4


def halves(array):
    high = array.astype(jnp.bfloat16)
    low = (array - high.astype(jnp.float32)).astype(jnp.bfloat16)
    return high, low


def tables(points):
    indices = np.arange(points)
    angles = 2.0 * np.pi * (np.outer(indices, indices) % points) / points
    pair = np.eye(2)
    along_z = np.concatenate([np.kron(pair, np.cos(angles)), np.kron(pair, np.sin(angles))], axis=1)
    half = points // 2
    short = np.arange(half)
    angles = 2.0 * np.pi * (np.outer(short, short) % half) / half
    planes = np.eye(SLAB)
    cosine, sine = np.kron(np.cos(angles), planes), np.kron(np.sin(angles), planes)
    along_y = np.block([[cosine, sine], [-sine, cosine]])
    turn = 2.0 * np.pi * np.repeat(short, SLAB) / points
    ones = np.ones((half * SLAB, points))
    twist = np.stack(
        [
            np.concatenate([ones, ones * np.cos(turn)[:, None]], axis=1),
            np.concatenate([0.0 * ones, ones * -np.sin(turn)[:, None]], axis=1),
        ]
    )

    return tuple(table.astype(np.float32) for table in (along_z, along_y, twist))


def unit_circle(steps, points):
    quarter = points // 4
    shifted = steps + quarter // 2
    turn = (shifted // quarter) & 3
    angle = ((shifted & (quarter - 1)) - quarter // 2).astype(jnp.float32) * (2.0 * math.pi / points)
    square = angle * angle
    sine = angle * (
        1.0 + square * (-1 / 6 + square * (1 / 120 + square * (-1 / 5040 + square * (1 / 362880))))
    )
    cosine = 1.0 + square * (
        -1 / 2
        + square * (1 / 24 + square * (-1 / 720 + square * (1 / 40320 - square * (1 / 3628800))))
    )
    odd = (turn & 1) == 1
    first = jnp.where(odd, sine, cosine)
    second = jnp.where(odd, cosine, sine)
    return (
        jnp.where((turn == 1) | (turn == 2), -first, first),
        jnp.where(turn >= 2, -second, second),
    )


def transform_kernel(
    points,
    valence_ids,
    conduct_ids,
    position,
    valence,
    conduction,
    envelope,
    grid_source,
    along_z_source,
    along_y_source,
    twist_source,
    out,
    left_rows,
    right_rows,
    common,
    grid,
    along_z,
    along_y,
    twist,
    field,
    waves,
    arrived,
):
    rows = points // 2 * SLAB
    blocks = out.shape[0] // 2
    tiles = grid.shape[0] // blocks
    dot = functools.partial(jnp.dot, preferred_element_type=jnp.float32)

    copies = []

    def fetch(source, target):
        copy = pltpu.make_async_copy(source, target, arrived.at[len(copies)])
        copy.start()
        copies.append(copy)
        return copy

    whole = [
        fetch(source, target)
        for source, target in (
            (grid_source, grid),
            (along_z_source, along_z),
            (envelope, common),
            (along_y_source, along_y),
            (twist_source, twist),
        )
    ]
    bands = []
    for t in range(COUNT):
        bands.append(
            (
                fetch(valence.at[:, valence_ids[t]], left_rows.at[t]),
                fetch(conduction.at[:, conduct_ids[t]], right_rows.at[t]),
            )
        )
    whole[0].wait()

    wave_x = grid[...] // (points * points)
    for plane in range(SLAB):
        steps = ((position[0] * SLAB + plane) * wave_x) & (points - 1)
        cosine, sine = unit_circle(steps, points)
        waves[2 * plane] = cosine
        waves[2 * plane + 1] = sine

    for copy in whole[1:]:
        copy.wait()
    z_high, z_low = halves(along_z[...])
    y_high, y_low = halves(along_y[...])

    common_real = common[0].astype(jnp.float32)
    common_imag = common[1].astype(jnp.float32)
    lane = lax.broadcasted_iota(jnp.int32, (rows, LANES), 1)
    sign = jnp.where(lane < points, 1.0, -1.0).astype(jnp.float32)
    for first in range(0, COUNT, 2):
        parts = []
        for t in (first, first + 1):
            for copy in bands[t]:
                copy.wait()
            left_real = left_rows[t, 0].astype(jnp.float32)
            left_imag = left_rows[t, 1].astype(jnp.float32)
            right_real = right_rows[t, 0].astype(jnp.float32) + common_real
            right_imag = right_rows[t, 1].astype(jnp.float32) + common_imag
            parts.append(left_real * right_real + left_imag * right_imag)
            parts.append(left_real * right_imag - left_imag * right_real)
        high, low = halves(jnp.concatenate(parts, axis=0))
        moved = dot(high, z_high) + (dot(low, z_high) + dot(high, z_low))
        columns = []
        for t in range(2):
            real = moved[2 * t * rows : (2 * t + 1) * rows]
            imag = moved[(2 * t + 1) * rows : (2 * t + 2) * rows]
            columns.append(
                jnp.concatenate(
                    [real[:, :LANES] + imag[:, LANES:], imag[:, :LANES] - real[:, LANES:]], axis=0
                )
            )
        high, low = halves(jnp.concatenate(columns, axis=1))
        moved = dot(y_high, high) + (dot(y_high, low) + dot(y_low, high))
        for t in range(2):
            real = moved[:rows, t * LANES : (t + 1) * LANES]
            imag = moved[rows:, t * LANES : (t + 1) * LANES]
            turned_real = real * twist[0] - imag * twist[1]
            turned_imag = real * twist[1] + imag * twist[0]
            start = (first + t) * rows
            field[0, start : start + rows] = pltpu.roll(turned_real, points, 1) + sign * turned_real
            field[1, start : start + rows] = pltpu.roll(turned_imag, points, 1) + sign * turned_imag

    half = blocks // 2
    left = lane[:COUNT] < points

    def one_pair(k, carry):
        picked = []
        for part in range(2):
            for y in range(SLAB):
                for x in range(SLAB):
                    start = (k * SLAB + y) * SLAB + x
                    picked.append(field[part, pl.ds(start, COUNT, stride=rows), :])
        high, low = halves(jnp.concatenate(picked, axis=0))
        source = jnp.concatenate([high, low], axis=1)
        chosen = []
        for side in range(2):
            row = (k + half * side) * tiles
            index = [grid[pl.ds(row + j, 1), :] for j in range(tiles)]
            depth = lax.broadcasted_iota(jnp.int32, (points, LANES), 0)
            match = jnp.concatenate(
                [jnp.where((i & (points - 1)) == depth, 1.0, 0.0) for i in index], axis=1
            ).astype(jnp.bfloat16)
            empty = jnp.zeros_like(match)
            order = [match, empty] if side == 0 else [empty, match]
            chosen.append(jnp.concatenate(order + order, axis=0))
        values = dot(source, jnp.concatenate(chosen, axis=1))
        for side in range(2):
            block = k + half * side
            for j in range(tiles):
                row = block * tiles + j
                at = (side * tiles + j) * LANES
                index = jnp.broadcast_to(grid[pl.ds(row, 1), :], (COUNT, LANES))
                wave_y = (index // points) & (SLAB - 1)
                total_real = jnp.zeros((COUNT, LANES), jnp.float32)
                total_imag = jnp.zeros((COUNT, LANES), jnp.float32)
                for x in range(SLAB):
                    pieces = []
                    for part in range(2):
                        of = [
                            values[((part * SLAB + y) * SLAB + x) * COUNT :][:COUNT, at : at + LANES]
                            for y in range(SLAB)
                        ]
                        pieces.append(
                            jnp.where(
                                wave_y < 2,
                                jnp.where(wave_y == 0, of[0], of[1]),
                                jnp.where(wave_y == 2, of[2], of[3]),
                            )
                        )
                    cosine = waves[2 * x, pl.ds(row, 1), :]
                    sine = waves[2 * x + 1, pl.ds(row, 1), :]
                    total_real += pieces[0] * cosine + pieces[1] * sine
                    total_imag += pieces[1] * cosine - pieces[0] * sine
                low = jnp.where(left, total_real, pltpu.roll(total_imag, points, 1))
                high = jnp.where(left, pltpu.roll(total_real, points, 1), total_imag)
                out[block, j * COUNT : (j + 1) * COUNT] = low
                out[blocks + block, j * COUNT : (j + 1) * COUNT] = high
        return carry

    lax.fori_loop(0, half, one_pair, 0)


def weight_kernel(scale, side, partial, coulomb, out):
    half = partial.shape[0] // 2
    lane = lax.broadcasted_iota(jnp.int32, (COUNT, LANES), 1)
    own = jnp.where(lane < LANES // 2, 0, 1) == (side[0] & 1)
    factors = []
    for j in range(partial.shape[1] // COUNT):
        root = jnp.sqrt(coulomb[:, j * LANES : (j + 1) * LANES])
        root = jnp.broadcast_to(root, (COUNT, LANES))
        factors.append(jnp.where(own, root, pltpu.roll(root, LANES // 2, 1)))
    factor = jnp.concatenate(factors, axis=0)
    pieces = []
    for first in (0, half):
        total = partial[first]
        for source in range(first + 1, first + half):
            total += partial[source]
        pieces.append((total * scale) * factor)
    weighted = jnp.concatenate(pieces, axis=0).astype(jnp.bfloat16)
    for target in range(out.shape[0]):
        out[target] = weighted


def panel_kernel(width, position, line_index, chip, gathered, out):
    line, group = line_index[0], (chip[0] >> 1) ^ ((position[0] >> 1) & 1)
    senders, height = gathered.shape[0], gathered.shape[1] // 2
    tiles = height // COUNT
    lane = lax.broadcasted_iota(jnp.int32, (1, LANES), 1)
    sign = jnp.where(lane < LANES // 2, -1.0, 1.0).astype(jnp.float32)

    def by_tile(array):
        shape = array.shape[:-2] + (2, tiles, COUNT, LANES)
        array = array.astype(jnp.float32).reshape(shape)
        return [array[..., j, :, :].reshape(-1, LANES) for j in range(tiles)]

    right = [tile.astype(jnp.bfloat16) for tile in by_tile(gathered[...])]
    rows = jnp.stack([gathered[2 * line + group], gathered[2 * line + 1 - group]])
    left = []
    for tile in by_tile(rows):
        turned = pltpu.roll(tile, LANES // 2, 1) * sign
        left.append(jnp.concatenate([tile, turned], axis=0).astype(jnp.bfloat16))
    total = lax.dot_general(
        jnp.concatenate(left, axis=1),
        jnp.concatenate(right, axis=1),
        (((1,), (1,)), ((), ())),
        preferred_element_type=jnp.float32,
    )
    out[...] = jnp.zeros_like(out)
    count = 4 * COUNT
    slot = 0
    for far in range(2):
        for side in range(2):
            start = (2 * far + side) * COUNT
            real = total[start : start + COUNT]
            imag = total[count + start : count + start + COUNT]
            for column in last_columns(out.shape[0] // 2, far):
                at = slice(column * width, (column + 1) * width)
                out[slot, :, :width] = real[:, at]
                out[slot, :, LANES // 2 : LANES // 2 + width] = imag[:, at]
                slot += 1


def sum_kernel(scale, partial, out):
    total = partial[0]
    for source in range(1, partial.shape[0]):
        total += partial[source]
    total *= scale
    width = out.shape[2]
    out[0] = total[:, :width]
    out[1] = total[:, LANES // 2 : LANES // 2 + width]


def last_columns(groups, far):
    return [g for g in range(groups) if (g // 2) % 2 == far]


def exchange(array, names, groups):
    return lax.all_to_all(
        array, names, split_axis=0, concat_axis=0, tiled=True, axis_index_groups=groups
    )


def body(valence, conduction, envelope, valence_index, conduction_index, grid_index, coulomb):
    points = math.isqrt(valence.shape[-1])
    groups, lines, chips = (lax.axis_size(name) for name in ("ga", "tr", "tc"))
    per_device = coulomb.shape[0]
    tiles = per_device // LANES
    rows = points // 2 * SLAB
    height = tiles * COUNT
    width = lines * chips * COUNT // groups

    def turned(array):
        lead = array.shape[:-2]
        split = array.reshape(lead + (SLAB, points // 2, LANES))
        return jnp.swapaxes(split, -3, -2).reshape(lead + (rows, LANES))

    position, line, chip = (
        lax.axis_index(name).astype(jnp.int32).reshape(1) for name in ("ga", "tr", "tc")
    )
    smem = pl.BlockSpec(memory_space=pltpu.SMEM)
    vmem = pl.BlockSpec(memory_space=pltpu.VMEM)
    anywhere = pl.BlockSpec(memory_space=pl.ANY)
    limit = pltpu.CompilerParams(vmem_limit_bytes=16 * 1024 * 1024)

    by_planes = [
        [(2 * high + low) * groups + g for low in range(2) for g in range(groups)]
        for high in range(chips // 2)
    ]
    by_rows = [
        [i * chips + 2 * high + low for i in range(lines) for high in range(chips // 2)]
        for low in range(2)
    ]
    by_columns = [
        [
            (2 * (high ^ far) + low) * groups + g
            for far in range(2)
            for low in range(2)
            for g in last_columns(groups, far)
        ]
        for high in range(chips // 2)
    ]

    along_z, along_y, twist = tables(points)
    partial = pl.pallas_call(
        functools.partial(transform_kernel, points),
        out_shape=jax.ShapeDtypeStruct((2 * groups, height, LANES), jnp.float32),
        in_specs=[smem] * 3 + [anywhere] * 7,
        out_specs=vmem,
        scratch_shapes=[
            pltpu.VMEM((COUNT, 2, rows, LANES), jnp.bfloat16),
            pltpu.VMEM((COUNT, 2, rows, LANES), jnp.bfloat16),
            pltpu.VMEM((2, rows, LANES), jnp.bfloat16),
            pltpu.VMEM((groups * tiles, LANES), jnp.int32),
            pltpu.VMEM(along_z.shape, jnp.float32),
            pltpu.VMEM(along_y.shape, jnp.float32),
            pltpu.VMEM(twist.shape, jnp.float32),
            pltpu.VMEM((2, COUNT * rows, LANES), jnp.float32),
            pltpu.VMEM((2 * SLAB, groups * tiles, LANES), jnp.float32),
            pltpu.SemaphoreType.DMA((5 + 2 * COUNT,)),
        ],
        compiler_params=pltpu.CompilerParams(vmem_limit_bytes=62 * 1024 * 1024),
        name="transform",
    )(
        valence_index,
        conduction_index,
        position,
        turned(valence),
        turned(conduction),
        turned(envelope),
        grid_index.reshape(groups * tiles, LANES),
        along_z,
        along_y,
        twist,
    )
    partial = exchange(partial, ("tc", "ga"), by_planes)
    copies = pl.pallas_call(
        functools.partial(weight_kernel, float(points) ** -1.5),
        out_shape=jax.ShapeDtypeStruct((lines * chips // 2, 2 * height, LANES), jnp.bfloat16),
        in_specs=[smem, vmem, vmem],
        out_specs=vmem,
        compiler_params=limit,
        name="weight",
    )(chip, partial, coulomb.reshape(1, per_device))
    gathered = exchange(copies, ("tr", "tc"), by_rows)
    terms = pl.pallas_call(
        functools.partial(panel_kernel, width),
        out_shape=jax.ShapeDtypeStruct((2 * groups, COUNT, LANES), jnp.float32),
        in_specs=[smem] * 3 + [vmem],
        out_specs=vmem,
        compiler_params=limit,
        name="panel",
    )(position, line, chip, gathered)
    terms = exchange(terms, ("tc", "ga"), by_columns)
    return pl.pallas_call(
        functools.partial(sum_kernel, 1.0 / (per_device * groups)),
        out_shape=jax.ShapeDtypeStruct((2, COUNT, width), jnp.float32),
        in_specs=[vmem],
        out_specs=vmem,
        compiler_params=limit,
        name="total",
    )(terms)


def solution(mesh):
    placed = (
        P(None, None, "ga", None),
        P(None, None, "ga", None),
        P(None, "ga", None),
        P(("tr", "tc")),
        P(("tr", "tc")),
        P(),
        P("ga"),
    )
    return jax.shard_map(
        body, mesh=mesh, in_specs=placed, out_specs=P(None, ("tr", "tc"), "ga"), check_vma=False
    )
```

```python
import functools
import math

import jax
import jax.numpy as jnp
import numpy as np
from jax import lax
from jax.experimental import pallas as pl
from jax.experimental.pallas import tpu as pltpu
from jax.sharding import PartitionSpec as P

LANES = 128
COUNT = 8
SLAB = 4


def halves(array):
    high = array.astype(jnp.bfloat16)
    low = (array - high.astype(jnp.float32)).astype(jnp.bfloat16)
    return high, low


def tables(points):
    indices = np.arange(points)
    angles = 2.0 * np.pi * (np.outer(indices, indices) % points) / points
    pair = np.eye(2)
    along_z = np.concatenate([np.kron(pair, np.cos(angles)), np.kron(pair, np.sin(angles))], axis=1)
    half = points // 2
    short = np.arange(half)
    angles = 2.0 * np.pi * (np.outer(short, short) % half) / half
    planes = np.eye(SLAB)
    cosine, sine = np.kron(np.cos(angles), planes), np.kron(np.sin(angles), planes)
    along_y = np.block([[cosine, sine], [-sine, cosine]])
    turn = 2.0 * np.pi * np.repeat(short, SLAB) / points
    ones = np.ones((half * SLAB, points))
    twist = np.stack(
        [
            np.concatenate([ones, ones * np.cos(turn)[:, None]], axis=1),
            np.concatenate([0.0 * ones, ones * -np.sin(turn)[:, None]], axis=1),
        ]
    )

    return tuple(table.astype(np.float32) for table in (along_z, along_y, twist))


def unit_circle(steps, points):
    quarter = points // 4
    shifted = steps + quarter // 2
    turn = (shifted // quarter) & 3
    angle = ((shifted & (quarter - 1)) - quarter // 2).astype(jnp.float32) * (2.0 * math.pi / points)
    square = angle * angle
    sine = angle * (
        1.0 + square * (-1 / 6 + square * (1 / 120 + square * (-1 / 5040 + square * (1 / 362880))))
    )
    cosine = 1.0 + square * (
        -1 / 2
        + square * (1 / 24 + square * (-1 / 720 + square * (1 / 40320 - square * (1 / 3628800))))
    )
    odd = (turn & 1) == 1
    first = jnp.where(odd, sine, cosine)
    second = jnp.where(odd, cosine, sine)
    return (
        jnp.where((turn == 1) | (turn == 2), -first, first),
        jnp.where(turn >= 2, -second, second),
    )


def transform_kernel(
    points,
    valence_ids,
    conduct_ids,
    position,
    valence,
    conduction,
    envelope,
    grid_source,
    along_z_source,
    along_y_source,
    twist_source,
    out,
    left_rows,
    right_rows,
    common,
    grid,
    along_z,
    along_y,
    twist,
    field,
    waves,
    powers,
    arrived,
):
    rows = points // 2 * SLAB
    blocks = out.shape[0] // 2
    tiles = grid.shape[0] // blocks
    dot = functools.partial(jnp.dot, preferred_element_type=jnp.float32)

    copies = []

    def fetch(source, target):
        copy = pltpu.make_async_copy(source, target, arrived.at[len(copies)])
        copy.start()
        copies.append(copy)
        return copy

    whole = [
        fetch(source, target)
        for source, target in (
            (grid_source, grid),
            (along_z_source, along_z),
            (envelope, common),
            (along_y_source, along_y),
            (twist_source, twist),
        )
    ]
    bands = []
    for t in range(COUNT):
        bands.append(
            (
                fetch(valence.at[:, valence_ids[t]], left_rows.at[t]),
                fetch(conduction.at[:, conduct_ids[t]], right_rows.at[t]),
            )
        )
    whole[0].wait()

    wave_x = grid[...] // (points * points)
    for plane in range(SLAB):
        steps = ((position[0] * SLAB + plane) * wave_x) & (points - 1)
        cosine, sine = unit_circle(steps, points)
        waves[2 * plane] = cosine
        waves[2 * plane + 1] = sine

    for copy in whole[1:]:
        copy.wait()
    z_high, z_low = halves(along_z[...])
    z_both = jnp.concatenate([z_high, z_high], axis=0)
    y_high, y_low = halves(along_y[...])

    common_real = common[0].astype(jnp.float32)
    common_imag = common[1].astype(jnp.float32)
    lane = lax.broadcasted_iota(jnp.int32, (rows, LANES), 1)
    sign = jnp.where(lane < points, 1.0, -1.0).astype(jnp.float32)
    for first in range(0, COUNT, 2):
        parts = []
        for t in (first, first + 1):
            for copy in bands[t]:
                copy.wait()
            left_real = left_rows[t, 0].astype(jnp.float32)
            left_imag = left_rows[t, 1].astype(jnp.float32)
            right_real = right_rows[t, 0].astype(jnp.float32) + common_real
            right_imag = right_rows[t, 1].astype(jnp.float32) + common_imag
            parts.append(left_real * right_real + left_imag * right_imag)
            parts.append(left_real * right_imag - left_imag * right_real)
            peak = jnp.max(jnp.maximum(jnp.abs(parts[-2]), jnp.abs(parts[-1])), axis=0, keepdims=True)
            peak = jnp.max(peak, axis=1, keepdims=True)
            power = jnp.clip(jnp.ceil(jnp.log2(peak)), -120.0, 120.0)
            powers[t : t + 1] = jnp.broadcast_to(power, (1, LANES))
        high, low = halves(jnp.concatenate(parts, axis=0))
        moved = dot(jnp.concatenate([high, low], axis=1), z_both) + dot(high, z_low)
        columns = []
        for t in range(2):
            real = moved[2 * t * rows : (2 * t + 1) * rows]
            imag = moved[(2 * t + 1) * rows : (2 * t + 2) * rows]
            columns.append(
                jnp.concatenate(
                    [real[:, :LANES] + imag[:, LANES:], imag[:, :LANES] - real[:, LANES:]], axis=0
                )
            )
        high, low = halves(jnp.concatenate(columns, axis=1))
        moved = dot(y_high, high) + (dot(y_high, low) + dot(y_low, high))
        for t in range(2):
            real = moved[:rows, t * LANES : (t + 1) * LANES]
            imag = moved[rows:, t * LANES : (t + 1) * LANES]
            turned_real = real * twist[0] - imag * twist[1]
            turned_imag = real * twist[1] + imag * twist[0]
            start = (first + t) * rows
            field[0, start : start + rows] = pltpu.roll(turned_real, points, 1) + sign * turned_real
            field[1, start : start + rows] = pltpu.roll(turned_imag, points, 1) + sign * turned_imag

    half = blocks // 2
    left = lane[:COUNT] < points
    depth = lax.broadcasted_iota(jnp.int32, (SLAB * points, LANES), 0)
    scale = jnp.exp2(-powers[...])
    last = tiles * COUNT
    for target in range(out.shape[0]):
        out[target, last : last + COUNT] = powers[...]

    def one_pair(k, carry):
        sources = ([], [])
        for part in range(2):
            for x in range(SLAB):
                lines = []
                for y in range(SLAB):
                    start = (k * SLAB + y) * SLAB + x
                    lines.append(field[part, pl.ds(start, COUNT, stride=rows), :])
                turned = [pltpu.roll(line, points, 1) for line in lines]
                sources[0].append(
                    jnp.concatenate(
                        [jnp.where(left, lines[y], turned[y + 1]) for y in range(0, SLAB, 2)], axis=1
                    )
                )
                sources[1].append(
                    jnp.concatenate(
                        [jnp.where(left, turned[y], lines[y + 1]) for y in range(0, SLAB, 2)], axis=1
                    )
                )
        for side in range(2):
            block = k + half * side
            high, low = halves(jnp.concatenate(sources[side], axis=0))
            match = []
            for j in range(tiles):
                index = grid[pl.ds(block * tiles + j, 1), :] & (SLAB * points - 1)
                match.append(jnp.where(index == depth, 1.0, 0.0).astype(jnp.bfloat16))
            match = jnp.concatenate(match, axis=1)
            values = dot(jnp.concatenate([high, low], axis=0), match)
            count = 2 * SLAB * COUNT
            values = values[:count] + values[count:]
            for j in range(tiles):
                row = block * tiles + j
                at = slice(j * LANES, (j + 1) * LANES)
                total_real = jnp.zeros((COUNT, LANES), jnp.float32)
                total_imag = jnp.zeros((COUNT, LANES), jnp.float32)
                for x in range(SLAB):
                    real = values[x * COUNT : (x + 1) * COUNT, at]
                    imag = values[(SLAB + x) * COUNT : (SLAB + x + 1) * COUNT, at]
                    cosine = waves[2 * x, pl.ds(row, 1), :]
                    sine = waves[2 * x + 1, pl.ds(row, 1), :]
                    total_real += real * cosine + imag * sine
                    total_imag += imag * cosine - real * sine
                total_real *= scale
                total_imag *= scale
                first = jnp.where(left, total_real, pltpu.roll(total_imag, points, 1))
                second = jnp.where(left, pltpu.roll(total_real, points, 1), total_imag)
                out[block, j * COUNT : (j + 1) * COUNT] = first
                out[blocks + block, j * COUNT : (j + 1) * COUNT] = second
        return carry

    lax.fori_loop(0, half, one_pair, 0)


def weight_kernel(scale, side, partial, coulomb, out):
    half = partial.shape[0] // 2
    lane = lax.broadcasted_iota(jnp.int32, (COUNT, LANES), 1)
    own = jnp.where(lane < LANES // 2, 0, 1) == (side[0] & 1)
    factors = []
    last = partial.shape[1] - COUNT
    for j in range(last // COUNT):
        root = jnp.sqrt(coulomb[:, j * LANES : (j + 1) * LANES])
        root = jnp.broadcast_to(root, (COUNT, LANES))
        factors.append(jnp.where(own, root, pltpu.roll(root, LANES // 2, 1)))
    factor = jnp.concatenate(factors, axis=0)
    pieces = []
    for first in (0, half):
        total = jnp.zeros((last, LANES), jnp.float32)
        for source in range(first, first + half):
            power = jnp.exp2(partial[source, last:])
            total += partial[source, :last] * jnp.concatenate([power] * (last // COUNT), axis=0)
        pieces.append((total * scale) * factor)
    weighted = jnp.concatenate(pieces, axis=0).astype(jnp.bfloat16)
    for target in range(out.shape[0]):
        out[target] = weighted


def panel_kernel(width, position, line_index, chip, gathered, out, terms):
    line, group = line_index[0], (chip[0] >> 1) ^ ((position[0] >> 1) & 1)
    senders, height = gathered.shape[0], gathered.shape[1] // 2
    tiles = height // COUNT
    lane = lax.broadcasted_iota(jnp.int32, (1, LANES), 1)
    sign = jnp.where(lane < LANES // 2, -1.0, 1.0).astype(jnp.float32)

    def by_tile(array):
        shape = array.shape[:-2] + (2, tiles, COUNT, LANES)
        array = array.astype(jnp.float32).reshape(shape)
        return [array[..., j, :, :].reshape(-1, LANES) for j in range(tiles)]

    right = [tile.astype(jnp.bfloat16) for tile in by_tile(gathered[...])]
    rows = jnp.stack([gathered[2 * line + group], gathered[2 * line + 1 - group]])
    left = []
    for tile in by_tile(rows):
        turned = pltpu.roll(tile, LANES // 2, 1) * sign
        left.append(jnp.concatenate([tile, turned], axis=0).astype(jnp.bfloat16))
    total = lax.dot_general(
        jnp.concatenate(left, axis=1),
        jnp.concatenate(right, axis=1),
        (((1,), (1,)), ((), ())),
        preferred_element_type=jnp.float32,
    )
    span = terms.shape[2]
    for tile in range(terms.shape[0]):
        terms[tile] = total[:, tile * span : (tile + 1) * span]
    slots = {}
    for far in range(2):
        for side in range(2):
            for column in last_columns(out.shape[0] // 2, far):
                slots[column, 2 * far + side] = len(slots)
    rows = [
        [terms[tile, pl.ds(a, 2 * 4, stride=COUNT), :] for a in range(COUNT)]
        for tile in range(terms.shape[0])
    ]
    for column in range(out.shape[0] // 2):
        tile, start = divmod(column * width, span)
        at = slice(start, start + width)
        line = jnp.concatenate([row[:, at] for row in rows[tile]], axis=1)
        for which in range(4):
            if (column, which) in slots:
                for part in range(2):
                    at = 4 * part + which
                    out[slots[column, which], part : part + 1] = line[at : at + 1]


def sum_kernel(scale, partial, out):
    total = partial[0]
    for source in range(1, partial.shape[0]):
        total += partial[source]
    total *= scale
    width = out.shape[2]
    for row in range(COUNT):
        out[:, row] = total[:, row * width : (row + 1) * width]


def last_columns(groups, far):
    return [g for g in range(groups) if (g // 2) % 2 == far]


def exchange(array, names, groups):
    return lax.all_to_all(
        array, names, split_axis=0, concat_axis=0, tiled=True, axis_index_groups=groups
    )


def body(valence, conduction, envelope, valence_index, conduction_index, grid_index, coulomb):
    points = math.isqrt(valence.shape[-1])
    groups, lines, chips = (lax.axis_size(name) for name in ("ga", "tr", "tc"))
    per_device = coulomb.shape[0]
    tiles = per_device // LANES
    rows = points // 2 * SLAB
    height = tiles * COUNT
    columns = lines * chips * COUNT
    width, span = columns // groups, min(columns, LANES)

    def turned(array):
        lead = array.shape[:-2]
        split = array.reshape(lead + (SLAB, points // 2, LANES))
        return jnp.swapaxes(split, -3, -2).reshape(lead + (rows, LANES))

    position, line, chip = (
        lax.axis_index(name).astype(jnp.int32).reshape(1) for name in ("ga", "tr", "tc")
    )
    smem = pl.BlockSpec(memory_space=pltpu.SMEM)
    vmem = pl.BlockSpec(memory_space=pltpu.VMEM)
    anywhere = pl.BlockSpec(memory_space=pl.ANY)
    limit = pltpu.CompilerParams(vmem_limit_bytes=16 * 1024 * 1024)

    by_planes = [
        [(2 * high + low) * groups + g for low in range(2) for g in range(groups)]
        for high in range(chips // 2)
    ]
    by_rows = [
        [i * chips + 2 * high + low for i in range(lines) for high in range(chips // 2)]
        for low in range(2)
    ]
    by_columns = [
        [
            (2 * (high ^ far) + low) * groups + g
            for far in range(2)
            for low in range(2)
            for g in last_columns(groups, far)
        ]
        for high in range(chips // 2)
    ]

    along_z, along_y, twist = tables(points)
    partial = pl.pallas_call(
        functools.partial(transform_kernel, points),
        out_shape=jax.ShapeDtypeStruct((2 * groups, height + COUNT, LANES), jnp.float32),
        in_specs=[smem] * 3 + [anywhere] * 7,
        out_specs=vmem,
        scratch_shapes=[
            pltpu.VMEM((COUNT, 2, rows, LANES), jnp.bfloat16),
            pltpu.VMEM((COUNT, 2, rows, LANES), jnp.bfloat16),
            pltpu.VMEM((2, rows, LANES), jnp.bfloat16),
            pltpu.VMEM((groups * tiles, LANES), jnp.int32),
            pltpu.VMEM(along_z.shape, jnp.float32),
            pltpu.VMEM(along_y.shape, jnp.float32),
            pltpu.VMEM(twist.shape, jnp.float32),
            pltpu.VMEM((2, COUNT * rows, LANES), jnp.float32),
            pltpu.VMEM((2 * SLAB, groups * tiles, LANES), jnp.float32),
            pltpu.VMEM((COUNT, LANES), jnp.float32),
            pltpu.SemaphoreType.DMA((5 + 2 * COUNT,)),
        ],
        compiler_params=pltpu.CompilerParams(vmem_limit_bytes=62 * 1024 * 1024),
        name="transform",
    )(
        valence_index,
        conduction_index,
        position,
        turned(valence),
        turned(conduction),
        turned(envelope),
        grid_index.reshape(groups * tiles, LANES),
        along_z,
        along_y,
        twist,
    )
    partial = exchange(partial.astype(jnp.float16), ("tc", "ga"), by_planes).astype(jnp.float32)
    copies = pl.pallas_call(
        functools.partial(weight_kernel, float(points) ** -1.5),
        out_shape=jax.ShapeDtypeStruct((lines * chips // 2, 2 * height, LANES), jnp.bfloat16),
        in_specs=[smem, vmem, vmem],
        out_specs=vmem,
        compiler_params=limit,
        name="weight",
    )(chip, partial, coulomb.reshape(1, per_device))
    gathered = exchange(copies, ("tr", "tc"), by_rows)
    terms = pl.pallas_call(
        functools.partial(panel_kernel, width),
        out_shape=jax.ShapeDtypeStruct((2 * groups, 2, COUNT * width), jnp.float32),
        in_specs=[smem] * 3 + [vmem],
        out_specs=vmem,
        scratch_shapes=[pltpu.VMEM((columns // span, 2 * 4 * COUNT, span), jnp.float32)],
        compiler_params=limit,
        name="panel",
    )(position, line, chip, gathered)
    terms = exchange(terms, ("tc", "ga"), by_columns)
    return pl.pallas_call(
        functools.partial(sum_kernel, 1.0 / (per_device * groups)),
        out_shape=jax.ShapeDtypeStruct((2, COUNT, width), jnp.float32),
        in_specs=[vmem],
        out_specs=vmem,
        compiler_params=limit,
        name="total",
    )(terms)


def solution(mesh):
    placed = (
        P(None, None, "ga", None),
        P(None, None, "ga", None),
        P(None, "ga", None),
        P(("tr", "tc")),
        P(("tr", "tc")),
        P(),
        P("ga"),
    )
    return jax.shard_map(
        body, mesh=mesh, in_specs=placed, out_specs=P(None, ("tr", "tc"), "ga"), check_vma=False
    )
```

```python
import functools
import math

import jax
import jax.numpy as jnp
import numpy as np
from jax import lax
from jax.experimental import pallas as pl
from jax.experimental.pallas import tpu as pltpu
from jax.sharding import PartitionSpec as P

LANES = 128
COUNT = 8
SLAB = 4


def halves(array):
    high = array.astype(jnp.bfloat16)
    low = (array - high.astype(jnp.float32)).astype(jnp.bfloat16)
    return high, low


def tables(points):
    indices = np.arange(points)
    angles = 2.0 * np.pi * (np.outer(indices, indices) % points) / points
    pair = np.eye(2)
    along_z = np.concatenate([np.kron(pair, np.cos(angles)), np.kron(pair, np.sin(angles))], axis=1)
    half = points // 2
    short = np.arange(half)
    angles = 2.0 * np.pi * (np.outer(short, short) % half) / half
    planes = np.eye(SLAB)
    cosine, sine = np.kron(np.cos(angles), planes), np.kron(np.sin(angles), planes)
    along_y = np.block([[cosine, sine], [-sine, cosine]])
    turn = 2.0 * np.pi * np.repeat(short, SLAB) / points
    ones = np.ones((half * SLAB, points))
    twist = np.stack(
        [
            np.concatenate([ones, ones * np.cos(turn)[:, None]], axis=1),
            np.concatenate([0.0 * ones, ones * -np.sin(turn)[:, None]], axis=1),
        ]
    )

    return tuple(table.astype(np.float32) for table in (along_z, along_y, twist))


def unit_circle(steps, points):
    quarter = points // 4
    shifted = steps + quarter // 2
    turn = (shifted // quarter) & 3
    angle = ((shifted & (quarter - 1)) - quarter // 2).astype(jnp.float32) * (2.0 * math.pi / points)
    square = angle * angle
    sine = angle * (
        1.0 + square * (-1 / 6 + square * (1 / 120 + square * (-1 / 5040 + square * (1 / 362880))))
    )
    cosine = 1.0 + square * (
        -1 / 2
        + square * (1 / 24 + square * (-1 / 720 + square * (1 / 40320 - square * (1 / 3628800))))
    )
    odd = (turn & 1) == 1
    first = jnp.where(odd, sine, cosine)
    second = jnp.where(odd, cosine, sine)
    return (
        jnp.where((turn == 1) | (turn == 2), -first, first),
        jnp.where(turn >= 2, -second, second),
    )


def transform_kernel(
    points,
    valence_ids,
    conduct_ids,
    position,
    valence,
    conduction,
    envelope,
    grid_source,
    along_z_source,
    along_y_source,
    twist_source,
    out,
    left_rows,
    right_rows,
    common,
    grid,
    along_z,
    along_y,
    twist,
    field,
    waves,
    powers,
    arrived,
):
    rows = points // 2 * SLAB
    blocks = out.shape[0] // 2
    tiles = grid.shape[0] // blocks
    dot = functools.partial(jnp.dot, preferred_element_type=jnp.float32)

    copies = []

    def fetch(source, target):
        copy = pltpu.make_async_copy(source, target, arrived.at[len(copies)])
        copy.start()
        copies.append(copy)
        return copy

    whole = [
        fetch(source, target)
        for source, target in (
            (grid_source, grid),
            (along_z_source, along_z),
            (envelope, common),
            (along_y_source, along_y),
            (twist_source, twist),
        )
    ]
    bands = []
    for t in range(COUNT):
        bands.append(
            (
                fetch(valence.at[:, valence_ids[t]], left_rows.at[t]),
                fetch(conduction.at[:, conduct_ids[t]], right_rows.at[t]),
            )
        )
    whole[0].wait()

    wave_x = grid[...] // (points * points)
    for plane in range(SLAB):
        steps = ((position[0] * SLAB + plane) * wave_x) & (points - 1)
        cosine, sine = unit_circle(steps, points)
        waves[2 * plane] = cosine
        waves[2 * plane + 1] = sine

    for copy in whole[1:]:
        copy.wait()
    z_high, z_low = halves(along_z[...])
    z_both = jnp.concatenate([z_high, z_high], axis=0)
    y_high, y_low = halves(along_y[...])

    common_real = common[0].astype(jnp.float32)
    common_imag = common[1].astype(jnp.float32)
    lane = lax.broadcasted_iota(jnp.int32, (rows, LANES), 1)
    sign = jnp.where(lane < points, 1.0, -1.0).astype(jnp.float32)
    for first in range(0, COUNT, 2):
        if first % 4 == 0:
            for pair in bands[first : first + 4]:
                for copy in pair:
                    copy.wait()
        parts = []
        for t in (first, first + 1):
            left_real = left_rows[t, 0].astype(jnp.float32)
            left_imag = left_rows[t, 1].astype(jnp.float32)
            right_real = right_rows[t, 0].astype(jnp.float32) + common_real
            right_imag = right_rows[t, 1].astype(jnp.float32) + common_imag
            parts.append(left_real * right_real + left_imag * right_imag)
            parts.append(left_real * right_imag - left_imag * right_real)
            peak = jnp.max(jnp.maximum(jnp.abs(parts[-2]), jnp.abs(parts[-1])), axis=0, keepdims=True)
            peak = jnp.max(peak, axis=1, keepdims=True)
            power = jnp.clip(jnp.ceil(jnp.log2(peak)), -120.0, 120.0)
            powers[t : t + 1] = jnp.broadcast_to(power, (1, LANES))
        high, low = halves(jnp.concatenate(parts, axis=0))
        moved = dot(jnp.concatenate([high, low], axis=1), z_both) + dot(high, z_low)
        columns = []
        for t in range(2):
            real = moved[2 * t * rows : (2 * t + 1) * rows]
            imag = moved[(2 * t + 1) * rows : (2 * t + 2) * rows]
            columns.append(
                jnp.concatenate(
                    [real[:, :LANES] + imag[:, LANES:], imag[:, :LANES] - real[:, LANES:]], axis=0
                )
            )
        high, low = halves(jnp.concatenate(columns, axis=1))
        moved = dot(y_high, high) + (dot(y_high, low) + dot(y_low, high))
        for t in range(2):
            real = moved[:rows, t * LANES : (t + 1) * LANES]
            imag = moved[rows:, t * LANES : (t + 1) * LANES]
            turned_real = real * twist[0] - imag * twist[1]
            turned_imag = real * twist[1] + imag * twist[0]
            start = (first + t) * rows
            field[0, start : start + rows] = pltpu.roll(turned_real, points, 1) + sign * turned_real
            field[1, start : start + rows] = pltpu.roll(turned_imag, points, 1) + sign * turned_imag

    half = blocks // 2
    left = lane[:COUNT] < points
    depth = lax.broadcasted_iota(jnp.int32, (SLAB * points, LANES), 0)
    scale = jnp.exp2(-powers[...])
    last = tiles * COUNT
    for target in range(out.shape[0]):
        out[target, last : last + COUNT] = powers[...]

    def one_pair(k, carry):
        sources = ([], [])
        for part in range(2):
            for x in range(SLAB):
                lines = []
                for y in range(SLAB):
                    start = (k * SLAB + y) * SLAB + x
                    lines.append(field[part, pl.ds(start, COUNT, stride=rows), :])
                turned = [pltpu.roll(line, points, 1) for line in lines]
                sources[0].append(
                    jnp.concatenate(
                        [jnp.where(left, lines[y], turned[y + 1]) for y in range(0, SLAB, 2)], axis=1
                    )
                )
                sources[1].append(
                    jnp.concatenate(
                        [jnp.where(left, turned[y], lines[y + 1]) for y in range(0, SLAB, 2)], axis=1
                    )
                )
        for side in range(2):
            block = k + half * side
            high, low = halves(jnp.concatenate(sources[side], axis=0))
            match = []
            for j in range(tiles):
                index = grid[pl.ds(block * tiles + j, 1), :] & (SLAB * points - 1)
                match.append(jnp.where(index == depth, 1.0, 0.0).astype(jnp.bfloat16))
            match = jnp.concatenate(match, axis=1)
            values = dot(jnp.concatenate([high, low], axis=0), match)
            count = 2 * SLAB * COUNT
            values = values[:count] + values[count:]
            for j in range(tiles):
                row = block * tiles + j
                at = slice(j * LANES, (j + 1) * LANES)
                total_real = jnp.zeros((COUNT, LANES), jnp.float32)
                total_imag = jnp.zeros((COUNT, LANES), jnp.float32)
                for x in range(SLAB):
                    real = values[x * COUNT : (x + 1) * COUNT, at]
                    imag = values[(SLAB + x) * COUNT : (SLAB + x + 1) * COUNT, at]
                    cosine = waves[2 * x, pl.ds(row, 1), :]
                    sine = waves[2 * x + 1, pl.ds(row, 1), :]
                    total_real += real * cosine + imag * sine
                    total_imag += imag * cosine - real * sine
                total_real *= scale
                total_imag *= scale
                first = jnp.where(left, total_real, pltpu.roll(total_imag, points, 1))
                second = jnp.where(left, pltpu.roll(total_real, points, 1), total_imag)
                out[block, j * COUNT : (j + 1) * COUNT] = first
                out[blocks + block, j * COUNT : (j + 1) * COUNT] = second
        return carry

    lax.fori_loop(0, half, one_pair, 0, unroll=4)


def weight_kernel(scale, side, partial, coulomb, out):
    half = partial.shape[0] // 2
    lane = lax.broadcasted_iota(jnp.int32, (COUNT, LANES), 1)
    own = jnp.where(lane < LANES // 2, 0, 1) == (side[0] >> 1)
    factors = []
    last = partial.shape[1] - COUNT
    for j in range(last // COUNT):
        root = jnp.sqrt(coulomb[:, j * LANES : (j + 1) * LANES])
        root = jnp.broadcast_to(root, (COUNT, LANES))
        factors.append(jnp.where(own, root, pltpu.roll(root, LANES // 2, 1)))
    factor = jnp.concatenate(factors, axis=0)
    pieces = []
    for first in (0, half):
        total = jnp.zeros((last, LANES), jnp.float32)
        for source in range(first, first + half):
            power = jnp.exp2(partial[source, last:])
            total += partial[source, :last] * jnp.concatenate([power] * (last // COUNT), axis=0)
        pieces.append((total * scale) * factor)
    weighted = jnp.concatenate(pieces, axis=0).astype(jnp.bfloat16)
    for target in range(out.shape[0]):
        out[target] = weighted


def panel_kernel(width, position, line_index, chip, gathered, out, terms):
    line = line_index[0]
    parity = ((chip[0] >> 1) ^ chip[0] ^ (position[0] >> 1)) & 1
    senders, height = gathered.shape[0], gathered.shape[1] // 2
    tiles = height // COUNT
    lane = lax.broadcasted_iota(jnp.int32, (1, LANES), 1)
    sign = jnp.where(lane < LANES // 2, -1.0, 1.0).astype(jnp.float32)

    def by_tile(array):
        shape = array.shape[:-2] + (2, tiles, COUNT, LANES)
        array = array.astype(jnp.float32).reshape(shape)
        return [array[..., j, :, :] for j in range(tiles)]

    right = []
    for tile in by_tile(gathered[...]):
        order = [tile[2 * i + low, high] for i in range(senders // 2) for high in range(2) for low in range(2)]
        right.append(jnp.concatenate(order, axis=0).astype(jnp.bfloat16))
    near = by_tile(gathered[2 * line + parity])
    away = by_tile(gathered[2 * line + 1 - parity])
    left = []
    for j in range(tiles):
        order = [(near, away)[far ^ high][j][high] for far in range(2) for high in range(2)]
        tile = jnp.concatenate(order, axis=0)
        turned = pltpu.roll(tile, LANES // 2, 1) * sign
        left.append(jnp.concatenate([tile, turned], axis=0).astype(jnp.bfloat16))
    total = lax.dot_general(
        jnp.concatenate(left, axis=1),
        jnp.concatenate(right, axis=1),
        (((1,), (1,)), ((), ())),
        preferred_element_type=jnp.float32,
    )
    span = terms.shape[2]
    for tile in range(terms.shape[0]):
        terms[tile] = total[:, tile * span : (tile + 1) * span]
    slots = {}
    for far in range(2):
        for side in range(2):
            for column in last_columns(out.shape[0] // 2, far):
                slots[column, 2 * far + side] = len(slots)
    rows = [
        [terms[tile, pl.ds(a, 2 * 4, stride=COUNT), :] for a in range(COUNT)]
        for tile in range(terms.shape[0])
    ]
    for column in range(out.shape[0] // 2):
        tile, start = divmod(column * width, span)
        at = slice(start, start + width)
        line = jnp.concatenate([row[:, at] for row in rows[tile]], axis=1)
        for which in range(4):
            if (column, which) in slots:
                for part in range(2):
                    at = 4 * part + which
                    out[slots[column, which], part : part + 1] = line[at : at + 1]


def sum_kernel(scale, partial, out):
    total = partial[0]
    for source in range(1, partial.shape[0]):
        total += partial[source]
    total *= scale
    width = out.shape[2]
    for row in range(COUNT):
        out[:, row] = total[:, row * width : (row + 1) * width]


def last_columns(groups, far):
    return [g for g in range(groups) if (g // 2) % 2 == far]


def exchange(array, names, groups):
    return lax.all_to_all(
        array, names, split_axis=0, concat_axis=0, tiled=True, axis_index_groups=groups
    )


def body(valence, conduction, envelope, valence_index, conduction_index, grid_index, coulomb):
    points = math.isqrt(valence.shape[-1])
    groups, lines, chips = (lax.axis_size(name) for name in ("ga", "tr", "tc"))
    per_device = coulomb.shape[0]
    tiles = per_device // LANES
    rows = points // 2 * SLAB
    height = tiles * COUNT
    columns = lines * chips * COUNT
    width, span = columns // groups, min(columns, LANES)

    def turned(array):
        lead = array.shape[:-2]
        split = array.reshape(lead + (SLAB, points // 2, LANES))
        return jnp.swapaxes(split, -3, -2).reshape(lead + (rows, LANES))

    position, line, chip = (
        lax.axis_index(name).astype(jnp.int32).reshape(1) for name in ("ga", "tr", "tc")
    )
    smem = pl.BlockSpec(memory_space=pltpu.SMEM)
    vmem = pl.BlockSpec(memory_space=pltpu.VMEM)
    anywhere = pl.BlockSpec(memory_space=pl.ANY)
    limit = pltpu.CompilerParams(vmem_limit_bytes=16 * 1024 * 1024)

    by_planes = [
        [(2 * high + low) * groups + g for high in range(2) for g in range(groups)]
        for low in range(2)
    ]
    by_rows = [
        [i * chips + 2 * high + low for i in range(lines) for low in range(2)] for high in range(2)
    ]
    by_columns = [
        [
            (2 * high + (far ^ high ^ parity)) * groups + g
            for far in range(2)
            for high in range(2)
            for g in last_columns(groups, far)
        ]
        for parity in range(2)
    ]

    along_z, along_y, twist = tables(points)
    partial = pl.pallas_call(
        functools.partial(transform_kernel, points),
        out_shape=jax.ShapeDtypeStruct((2 * groups, height + COUNT, LANES), jnp.float32),
        in_specs=[smem] * 3 + [anywhere] * 7,
        out_specs=vmem,
        scratch_shapes=[
            pltpu.VMEM((COUNT, 2, rows, LANES), jnp.bfloat16),
            pltpu.VMEM((COUNT, 2, rows, LANES), jnp.bfloat16),
            pltpu.VMEM((2, rows, LANES), jnp.bfloat16),
            pltpu.VMEM((groups * tiles, LANES), jnp.int32),
            pltpu.VMEM(along_z.shape, jnp.float32),
            pltpu.VMEM(along_y.shape, jnp.float32),
            pltpu.VMEM(twist.shape, jnp.float32),
            pltpu.VMEM((2, COUNT * rows, LANES), jnp.float32),
            pltpu.VMEM((2 * SLAB, groups * tiles, LANES), jnp.float32),
            pltpu.VMEM((COUNT, LANES), jnp.float32),
            pltpu.SemaphoreType.DMA((5 + 2 * COUNT,)),
        ],
        compiler_params=pltpu.CompilerParams(vmem_limit_bytes=62 * 1024 * 1024),
        name="transform",
    )(
        valence_index,
        conduction_index,
        position,
        turned(valence),
        turned(conduction),
        turned(envelope),
        grid_index.reshape(groups * tiles, LANES),
        along_z,
        along_y,
        twist,
    )
    partial = exchange(partial.astype(jnp.float16), ("tc", "ga"), by_planes).astype(jnp.float32)
    copies = pl.pallas_call(
        functools.partial(weight_kernel, float(points) ** -1.5),
        out_shape=jax.ShapeDtypeStruct((lines * chips // 2, 2 * height, LANES), jnp.bfloat16),
        in_specs=[smem, vmem, vmem],
        out_specs=vmem,
        compiler_params=limit,
        name="weight",
    )(chip, partial, coulomb.reshape(1, per_device))
    gathered = exchange(copies, ("tr", "tc"), by_rows)
    terms = pl.pallas_call(
        functools.partial(panel_kernel, width),
        out_shape=jax.ShapeDtypeStruct((2 * groups, 2, COUNT * width), jnp.float32),
        in_specs=[smem] * 3 + [vmem],
        out_specs=vmem,
        scratch_shapes=[pltpu.VMEM((columns // span, 2 * 4 * COUNT, span), jnp.float32)],
        compiler_params=limit,
        name="panel",
    )(position, line, chip, gathered)
    terms = exchange(terms, ("tc", "ga"), by_columns)
    return pl.pallas_call(
        functools.partial(sum_kernel, 1.0 / (per_device * groups)),
        out_shape=jax.ShapeDtypeStruct((2, COUNT, width), jnp.float32),
        in_specs=[vmem],
        out_specs=vmem,
        compiler_params=limit,
        name="total",
    )(terms)


def solution(mesh):
    placed = (
        P(None, None, "ga", None),
        P(None, None, "ga", None),
        P(None, "ga", None),
        P(("tr", "tc")),
        P(("tr", "tc")),
        P(),
        P("ga"),
    )
    return jax.shard_map(
        body, mesh=mesh, in_specs=placed, out_specs=P(None, ("tr", "tc"), "ga"), check_vma=False
    )
```

```python
import functools
import math

import jax
import jax.numpy as jnp
import numpy as np
from jax import lax
from jax.experimental import pallas as pl
from jax.experimental.pallas import tpu as pltpu
from jax.sharding import PartitionSpec as P

LANES = 128
COUNT = 8
SLAB = 4


def halves(array):
    high = array.astype(jnp.bfloat16)
    low = (array - high.astype(jnp.float32)).astype(jnp.bfloat16)
    return high, low


def tables(points):
    indices = np.arange(points)
    angles = 2.0 * np.pi * (np.outer(indices, indices) % points) / points
    pair = np.eye(2)
    along_z = np.concatenate([np.kron(pair, np.cos(angles)), np.kron(pair, np.sin(angles))], axis=1)
    half = points // 2
    short = np.arange(half)
    angles = 2.0 * np.pi * (np.outer(short, short) % half) / half
    planes = np.eye(SLAB)
    cosine, sine = np.kron(np.cos(angles), planes), np.kron(np.sin(angles), planes)
    along_y = np.block([[cosine, sine], [-sine, cosine]])
    turn = 2.0 * np.pi * np.repeat(short, SLAB) / points
    ones = np.ones((half * SLAB, points))
    twist = np.stack(
        [
            np.concatenate([ones, ones * np.cos(turn)[:, None]], axis=1),
            np.concatenate([0.0 * ones, ones * -np.sin(turn)[:, None]], axis=1),
        ]
    )

    return tuple(table.astype(np.float32) for table in (along_z, along_y, twist))


def unit_circle(steps, points):
    quarter = points // 4
    shifted = steps + quarter // 2
    turn = (shifted // quarter) & 3
    angle = ((shifted & (quarter - 1)) - quarter // 2).astype(jnp.float32) * (2.0 * math.pi / points)
    square = angle * angle
    sine = angle * (
        1.0 + square * (-1 / 6 + square * (1 / 120 + square * (-1 / 5040 + square * (1 / 362880))))
    )
    cosine = 1.0 + square * (
        -1 / 2
        + square * (1 / 24 + square * (-1 / 720 + square * (1 / 40320 - square * (1 / 3628800))))
    )
    odd = (turn & 1) == 1
    first = jnp.where(odd, sine, cosine)
    second = jnp.where(odd, cosine, sine)
    return (
        jnp.where((turn == 1) | (turn == 2), -first, first),
        jnp.where(turn >= 2, -second, second),
    )


def transform_kernel(
    points,
    valence_ids,
    conduct_ids,
    valence,
    conduction,
    envelope,
    grid_source,
    along_z_source,
    along_y_source,
    twist_source,
    result,
    left_rows,
    right_rows,
    common,
    grid,
    along_z,
    along_y,
    twist,
    field,
    waves,
    powers,
    out,
    arrived,
    sent,
):
    rows = points // 2 * SLAB
    blocks = result.shape[0] // 2
    tiles = grid.shape[0] // blocks
    dot = functools.partial(jnp.dot, preferred_element_type=jnp.float32)

    copies = []

    def fetch(source, target):
        copy = pltpu.make_async_copy(source, target, arrived.at[len(copies)])
        copy.start()
        copies.append(copy)
        return copy

    for source, target in (
        (grid_source, grid),
        (along_z_source, along_z),
        (envelope, common),
        (along_y_source, along_y),
        (twist_source, twist),
    ):
        fetch(source, target)
    for t in range(COUNT):
        fetch(valence.at[:, valence_ids[t]], left_rows.at[t])
        fetch(conduction.at[:, conduct_ids[t]], right_rows.at[t])
    copies[0].wait()

    position = lax.axis_index("ga")
    wave_x = grid[...] // (points * points)
    for plane in range(SLAB):
        steps = ((position * SLAB + plane) * wave_x) & (points - 1)
        cosine, sine = unit_circle(steps, points)
        waves[2 * plane] = cosine
        waves[2 * plane + 1] = sine

    for copy in copies[1:]:
        copy.wait()

    z_high, z_low = halves(along_z[...])
    z_both = jnp.concatenate([z_high, z_high], axis=0)
    y_high, y_low = halves(along_y[...])

    common_real = common[0].astype(jnp.float32)
    common_imag = common[1].astype(jnp.float32)
    lane = lax.broadcasted_iota(jnp.int32, (rows, LANES), 1)
    sign = jnp.where(lane < points, 1.0, -1.0).astype(jnp.float32)
    for first in range(0, COUNT, 2):
        parts = []
        for t in (first, first + 1):
            left_real = left_rows[t, 0].astype(jnp.float32)
            left_imag = left_rows[t, 1].astype(jnp.float32)
            right_real = right_rows[t, 0].astype(jnp.float32) + common_real
            right_imag = right_rows[t, 1].astype(jnp.float32) + common_imag
            parts.append(left_real * right_real + left_imag * right_imag)
            parts.append(left_real * right_imag - left_imag * right_real)
            peak = jnp.max(jnp.maximum(jnp.abs(parts[-2]), jnp.abs(parts[-1])), axis=0, keepdims=True)
            peak = jnp.max(peak, axis=1, keepdims=True)
            power = jnp.clip(jnp.ceil(jnp.log2(peak)), -120.0, 120.0)
            powers[t : t + 1] = jnp.broadcast_to(power, (1, LANES))
        high, low = halves(jnp.concatenate(parts, axis=0))
        moved = dot(jnp.concatenate([high, low], axis=1), z_both) + dot(high, z_low)
        columns = []
        for t in range(2):
            real = moved[2 * t * rows : (2 * t + 1) * rows]
            imag = moved[(2 * t + 1) * rows : (2 * t + 2) * rows]
            columns.append(
                jnp.concatenate(
                    [real[:, :LANES] + imag[:, LANES:], imag[:, :LANES] - real[:, LANES:]], axis=0
                )
            )
        high, low = halves(jnp.concatenate(columns, axis=1))
        moved = dot(y_high, high) + (dot(y_high, low) + dot(y_low, high))
        for t in range(2):
            real = moved[:rows, t * LANES : (t + 1) * LANES]
            imag = moved[rows:, t * LANES : (t + 1) * LANES]
            turned_real = real * twist[0] - imag * twist[1]
            turned_imag = real * twist[1] + imag * twist[0]
            start = (first + t) * rows
            field[0, start : start + rows] = pltpu.roll(turned_real, points, 1) + sign * turned_real
            field[1, start : start + rows] = pltpu.roll(turned_imag, points, 1) + sign * turned_imag

    half = blocks // 2
    left = lane[:COUNT] < points
    depth = lax.broadcasted_iota(jnp.int32, (SLAB * points, LANES), 0)
    scale = jnp.exp2(-powers[...])
    last = tiles * COUNT
    for slot in range(out.shape[0]):
        out[slot, last : last + COUNT] = powers[...]

    copies = []
    for k in range(half):
        sources = ([], [])
        for part in range(2):
            for x in range(SLAB):
                lines = []
                for y in range(SLAB):
                    start = (k * SLAB + y) * SLAB + x
                    lines.append(field[part, pl.ds(start, COUNT, stride=rows), :])
                turned = [pltpu.roll(line, points, 1) for line in lines]
                sources[0].append(
                    jnp.concatenate(
                        [jnp.where(left, lines[y], turned[y + 1]) for y in range(0, SLAB, 2)], axis=1
                    )
                )
                sources[1].append(
                    jnp.concatenate(
                        [jnp.where(left, turned[y], lines[y + 1]) for y in range(0, SLAB, 2)], axis=1
                    )
                )
        for side in range(2):
            block = k + half * side
            high, low = halves(jnp.concatenate(sources[side], axis=0))
            match = []
            for j in range(tiles):
                index = grid[pl.ds(block * tiles + j, 1), :] & (SLAB * points - 1)
                match.append(jnp.where(index == depth, 1.0, 0.0).astype(jnp.bfloat16))
            match = jnp.concatenate(match, axis=1)
            values = dot(jnp.concatenate([high, low], axis=0), match)
            count = 2 * SLAB * COUNT
            values = values[:count] + values[count:]
            for j in range(tiles):
                row = block * tiles + j
                at = slice(j * LANES, (j + 1) * LANES)
                total_real = jnp.zeros((COUNT, LANES), jnp.float32)
                total_imag = jnp.zeros((COUNT, LANES), jnp.float32)
                for x in range(SLAB):
                    real = values[x * COUNT : (x + 1) * COUNT, at]
                    imag = values[(SLAB + x) * COUNT : (SLAB + x + 1) * COUNT, at]
                    cosine = waves[2 * x, pl.ds(row, 1), :]
                    sine = waves[2 * x + 1, pl.ds(row, 1), :]
                    total_real += real * cosine + imag * sine
                    total_imag += imag * cosine - real * sine
                total_real *= scale
                total_imag *= scale
                first = jnp.where(left, total_real, pltpu.roll(total_imag, points, 1))
                second = jnp.where(left, pltpu.roll(total_real, points, 1), total_imag)
                out[block, j * COUNT : (j + 1) * COUNT] = first
                out[blocks + block, j * COUNT : (j + 1) * COUNT] = second
            for slot in (block, blocks + block):
                copy = pltpu.make_async_copy(out.at[slot], result.at[slot], sent.at[slot])
                copy.start()
                copies.append(copy)
    for copy in copies:
        copy.wait()


def weight_kernel(scale, partial, coulomb, out):
    half = partial.shape[0] // 2
    last = partial.shape[1] - COUNT
    lane = lax.broadcasted_iota(jnp.int32, (COUNT, LANES), 1)
    own = jnp.where(lane < LANES // 2, 0, 1) == lax.axis_index("tc") // 2
    factors = []
    for j in range(last // COUNT):
        root = jnp.broadcast_to(jnp.sqrt(coulomb[j : j + 1]), (COUNT, LANES))
        factors.append(jnp.where(own, root, pltpu.roll(root, LANES // 2, 1)))
    factor = jnp.concatenate(factors, axis=0)
    pieces = []
    for first in (0, half):
        total = jnp.zeros((last, LANES), jnp.float32)
        for source in range(first, first + half):
            power = jnp.exp2(partial[source, last:])
            total += partial[source, :last] * jnp.concatenate([power] * (last // COUNT), axis=0)
        pieces.append((total * scale) * factor)
    weighted = jnp.concatenate(pieces, axis=0).astype(jnp.bfloat16)
    for target in range(out.shape[0]):
        out[target] = weighted


def panel_kernel(width, gathered, out, terms):
    line, chip = lax.axis_index("tr"), lax.axis_index("tc")
    parity = (chip // 2 + chip + lax.axis_index("ga") // 2) % 2
    senders, height = gathered.shape[0], gathered.shape[1] // 2
    tiles = height // COUNT
    lane = lax.broadcasted_iota(jnp.int32, (1, LANES), 1)
    sign = jnp.where(lane < LANES // 2, -1.0, 1.0).astype(jnp.float32)

    def by_tile(array):
        shape = array.shape[:-2] + (2, tiles, COUNT, LANES)
        array = array.astype(jnp.float32).reshape(shape)
        return [array[..., j, :, :] for j in range(tiles)]

    right = []
    for tile in by_tile(gathered[...]):
        order = [tile[2 * i + low, high] for i in range(senders // 2) for high in range(2) for low in range(2)]
        right.append(jnp.concatenate(order, axis=0).astype(jnp.bfloat16))
    near = by_tile(gathered[2 * line + parity])
    away = by_tile(gathered[2 * line + 1 - parity])
    left = []
    for j in range(tiles):
        order = [(near, away)[far ^ high][j][high] for far in range(2) for high in range(2)]
        tile = jnp.concatenate(order, axis=0)
        turned = pltpu.roll(tile, LANES // 2, 1) * sign
        left.append(jnp.concatenate([tile, turned], axis=0).astype(jnp.bfloat16))
    total = lax.dot_general(
        jnp.concatenate(left, axis=1),
        jnp.concatenate(right, axis=1),
        (((1,), (1,)), ((), ())),
        preferred_element_type=jnp.float32,
    )
    span = terms.shape[2]
    for tile in range(terms.shape[0]):
        terms[tile] = total[:, tile * span : (tile + 1) * span]
    slots = {}
    for far in range(2):
        for side in range(2):
            for column in last_columns(out.shape[0] // 2, far):
                slots[column, 2 * far + side] = len(slots)
    rows = [
        [terms[tile, pl.ds(a, 2 * 4, stride=COUNT), :] for a in range(COUNT)]
        for tile in range(terms.shape[0])
    ]
    for column in range(out.shape[0] // 2):
        tile, start = divmod(column * width, span)
        at = slice(start, start + width)
        line = jnp.concatenate([row[:, at] for row in rows[tile]], axis=1)
        for which in range(4):
            if (column, which) in slots:
                for part in range(2):
                    at = 4 * part + which
                    out[slots[column, which], part : part + 1] = line[at : at + 1]


def sum_kernel(scale, partial, out):
    total = partial[0]
    for source in range(1, partial.shape[0]):
        total += partial[source]
    total *= scale
    width = out.shape[2]
    for row in range(COUNT):
        out[:, row] = total[:, row * width : (row + 1) * width]


def last_columns(groups, far):
    return [g for g in range(groups) if (g // 2) % 2 == far]


def exchange(array, names, groups):
    return lax.all_to_all(
        array, names, split_axis=0, concat_axis=0, tiled=True, axis_index_groups=groups
    )


def body(valence, conduction, envelope, valence_index, conduction_index, grid_index, coulomb):
    points = math.isqrt(valence.shape[-1])
    groups, lines, chips = (lax.axis_size(name) for name in ("ga", "tr", "tc"))
    per_device = coulomb.shape[0]
    tiles = per_device // LANES
    rows = points // 2 * SLAB
    height = tiles * COUNT
    columns = lines * chips * COUNT
    width, span = columns // groups, min(columns, LANES)

    def turned(array):
        lead = array.shape[:-2]
        split = array.reshape(lead + (SLAB, points // 2, LANES))
        return jnp.swapaxes(split, -3, -2).reshape(lead + (rows, LANES))

    smem = pl.BlockSpec(memory_space=pltpu.SMEM)
    vmem = pl.BlockSpec(memory_space=pltpu.VMEM)
    hbm = pl.BlockSpec(memory_space=pl.ANY)
    limit = pltpu.CompilerParams(vmem_limit_bytes=16 * 1024 * 1024)

    by_planes = [
        [(2 * high + low) * groups + g for high in range(2) for g in range(groups)]
        for low in range(2)
    ]
    by_rows = [
        [i * chips + 2 * high + low for i in range(lines) for low in range(2)] for high in range(2)
    ]
    by_columns = [
        [
            (2 * high + (far ^ high ^ parity)) * groups + g
            for far in range(2)
            for high in range(2)
            for g in last_columns(groups, far)
        ]
        for parity in range(2)
    ]

    along_z, along_y, twist = tables(points)
    partial = pl.pallas_call(
        functools.partial(transform_kernel, points),
        out_shape=jax.ShapeDtypeStruct((2 * groups, height + COUNT, LANES), jnp.float32),
        in_specs=[smem] * 2 + [hbm] * 7,
        out_specs=hbm,
        scratch_shapes=[
            pltpu.VMEM((COUNT, 2, rows, LANES), jnp.bfloat16),
            pltpu.VMEM((COUNT, 2, rows, LANES), jnp.bfloat16),
            pltpu.VMEM((2, rows, LANES), jnp.bfloat16),
            pltpu.VMEM((groups * tiles, LANES), jnp.int32),
            pltpu.VMEM(along_z.shape, jnp.float32),
            pltpu.VMEM(along_y.shape, jnp.float32),
            pltpu.VMEM(twist.shape, jnp.float32),
            pltpu.VMEM((2, COUNT * rows, LANES), jnp.float32),
            pltpu.VMEM((2 * SLAB, groups * tiles, LANES), jnp.float32),
            pltpu.VMEM((COUNT, LANES), jnp.float32),
            pltpu.VMEM((2 * groups, height + COUNT, LANES), jnp.float32),
            pltpu.SemaphoreType.DMA((5 + 2 * COUNT,)),
            pltpu.SemaphoreType.DMA((2 * groups,)),
        ],
        compiler_params=pltpu.CompilerParams(vmem_limit_bytes=60 * 1024 * 1024),
        name="transform",
    )(
        valence_index,
        conduction_index,
        turned(valence),
        turned(conduction),
        turned(envelope),
        grid_index.reshape(groups * tiles, LANES),
        along_z,
        along_y,
        twist,
    )
    partial = exchange(partial.astype(jnp.float16), ("tc", "ga"), by_planes).astype(jnp.float32)
    copies = pl.pallas_call(
        functools.partial(weight_kernel, float(points) ** -1.5),
        out_shape=jax.ShapeDtypeStruct((lines * chips // 2, 2 * height, LANES), jnp.bfloat16),
        in_specs=[vmem, vmem],
        out_specs=vmem,
        compiler_params=limit,
        name="weight",
    )(partial, coulomb.reshape(tiles, LANES))
    gathered = exchange(copies, ("tr", "tc"), by_rows)
    terms = pl.pallas_call(
        functools.partial(panel_kernel, width),
        out_shape=jax.ShapeDtypeStruct((2 * groups, 2, COUNT * width), jnp.float32),
        in_specs=[vmem],
        out_specs=vmem,
        scratch_shapes=[pltpu.VMEM((columns // span, 2 * 4 * COUNT, span), jnp.float32)],
        compiler_params=limit,
        name="panel",
    )(gathered)
    terms = exchange(terms, ("tc", "ga"), by_columns)
    return pl.pallas_call(
        functools.partial(sum_kernel, 1.0 / (per_device * groups)),
        out_shape=jax.ShapeDtypeStruct((2, COUNT, width), jnp.float32),
        in_specs=[vmem],
        out_specs=vmem,
        compiler_params=limit,
        name="total",
    )(terms)


def solution(mesh):
    placed = (
        P(None, None, "ga", None),
        P(None, None, "ga", None),
        P(None, "ga", None),
        P(("tr", "tc")),
        P(("tr", "tc")),
        P(),
        P("ga"),
    )
    return jax.shard_map(
        body, mesh=mesh, in_specs=placed, out_specs=P(None, ("tr", "tc"), "ga"), check_vma=False
    )
```

```python
import functools
import math

import jax
import jax.numpy as jnp
import numpy as np
from jax import lax
from jax.experimental import pallas as pl
from jax.experimental.pallas import tpu as pltpu
from jax.sharding import PartitionSpec as P

LANES = 128
COUNT = 8
SLAB = 4


def halves(array):
    high = array.astype(jnp.bfloat16)
    low = (array - high.astype(jnp.float32)).astype(jnp.bfloat16)
    return high, low


def tables(points):
    indices = np.arange(points)
    angles = 2.0 * np.pi * (np.outer(indices, indices) % points) / points
    pair = np.eye(2)
    along_z = np.concatenate([np.kron(pair, np.cos(angles)), np.kron(pair, np.sin(angles))], axis=1)
    half = points // 2
    short = np.arange(half)
    angles = 2.0 * np.pi * (np.outer(short, short) % half) / half
    planes = np.eye(SLAB)
    cosine, sine = np.kron(np.cos(angles), planes), np.kron(np.sin(angles), planes)
    along_y = np.block([[cosine, sine], [-sine, cosine]])
    turn = 2.0 * np.pi * np.repeat(short, SLAB) / points
    ones = np.ones((half * SLAB, points))
    twist = np.stack(
        [
            np.concatenate([ones, ones * np.cos(turn)[:, None]], axis=1),
            np.concatenate([0.0 * ones, ones * -np.sin(turn)[:, None]], axis=1),
        ]
    )

    return tuple(table.astype(np.float32) for table in (along_z, along_y, twist))


def unit_circle(steps, points):
    quarter = points // 4
    shifted = steps + quarter // 2
    turn = (shifted // quarter) & 3
    angle = ((shifted & (quarter - 1)) - quarter // 2).astype(jnp.float32) * (2.0 * math.pi / points)
    square = angle * angle
    sine = angle * (
        1.0 + square * (-1 / 6 + square * (1 / 120 + square * (-1 / 5040 + square * (1 / 362880))))
    )
    cosine = 1.0 + square * (
        -1 / 2
        + square * (1 / 24 + square * (-1 / 720 + square * (1 / 40320 - square * (1 / 3628800))))
    )
    odd = (turn & 1) == 1
    first = jnp.where(odd, sine, cosine)
    second = jnp.where(odd, cosine, sine)
    return (
        jnp.where((turn == 1) | (turn == 2), -first, first),
        jnp.where(turn >= 2, -second, second),
    )


def transform_kernel(
    points,
    valence_ids,
    conduct_ids,
    valence,
    conduction,
    envelope,
    grid_source,
    along_z_source,
    along_y_source,
    twist_source,
    result,
    left_rows,
    right_rows,
    common,
    grid,
    along_z,
    along_y,
    twist,
    field,
    waves,
    powers,
    out,
    arrived,
    sent,
):
    rows = points // 2 * SLAB
    blocks = result.shape[0] // 2
    tiles = grid.shape[0] // blocks
    dot = functools.partial(jnp.dot, preferred_element_type=jnp.float32)

    copies = []

    def fetch(source, target):
        copy = pltpu.make_async_copy(source, target, arrived.at[len(copies)])
        copy.start()
        copies.append(copy)
        return copy

    for source, target in (
        (grid_source, grid),
        (along_z_source, along_z),
        (envelope, common),
        (along_y_source, along_y),
        (twist_source, twist),
    ):
        fetch(source, target)
    for t in range(COUNT):
        fetch(valence.at[:, valence_ids[t]], left_rows.at[t])
        fetch(conduction.at[:, conduct_ids[t]], right_rows.at[t])
    copies[0].wait()

    position = lax.axis_index("ga")
    wave_x = grid[...] // (points * points)
    for plane in range(SLAB):
        steps = ((position * SLAB + plane) * wave_x) & (points - 1)
        cosine, sine = unit_circle(steps, points)
        waves[2 * plane] = cosine
        waves[2 * plane + 1] = sine

    for copy in copies[1:]:
        copy.wait()

    z_high, z_low = halves(along_z[...])
    z_both = jnp.concatenate([z_high, z_high], axis=0)
    y_high, y_low = halves(along_y[...])

    common_real = common[0].astype(jnp.float32)
    common_imag = common[1].astype(jnp.float32)
    lane = lax.broadcasted_iota(jnp.int32, (rows, LANES), 1)
    sign = jnp.where(lane < points, 1.0, -1.0).astype(jnp.float32)
    for first in range(0, COUNT, 2):
        parts = []
        for t in (first, first + 1):
            left_real = left_rows[t, 0].astype(jnp.float32)
            left_imag = left_rows[t, 1].astype(jnp.float32)
            right_real = right_rows[t, 0].astype(jnp.float32) + common_real
            right_imag = right_rows[t, 1].astype(jnp.float32) + common_imag
            parts.append(left_real * right_real + left_imag * right_imag)
            parts.append(left_real * right_imag - left_imag * right_real)
            peak = jnp.max(jnp.maximum(jnp.abs(parts[-2]), jnp.abs(parts[-1])), axis=0, keepdims=True)
            peak = jnp.max(peak, axis=1, keepdims=True)
            power = jnp.clip(jnp.ceil(jnp.log2(peak)), -120.0, 120.0)
            powers[t : t + 1] = jnp.broadcast_to(power, (1, LANES))
        high, low = halves(jnp.concatenate(parts, axis=0))
        moved = dot(jnp.concatenate([high, low], axis=1), z_both) + dot(high, z_low)
        columns = []
        for t in range(2):
            real = moved[2 * t * rows : (2 * t + 1) * rows]
            imag = moved[(2 * t + 1) * rows : (2 * t + 2) * rows]
            columns.append(
                jnp.concatenate(
                    [real[:, :LANES] + imag[:, LANES:], imag[:, :LANES] - real[:, LANES:]], axis=0
                )
            )
        high, low = halves(jnp.concatenate(columns, axis=1))
        moved = dot(y_high, high) + (dot(y_high, low) + dot(y_low, high))
        for t in range(2):
            real = moved[:rows, t * LANES : (t + 1) * LANES]
            imag = moved[rows:, t * LANES : (t + 1) * LANES]
            turned_real = real * twist[0] - imag * twist[1]
            turned_imag = real * twist[1] + imag * twist[0]
            start = (first + t) * rows
            field[0, start : start + rows] = pltpu.roll(turned_real, points, 1) + sign * turned_real
            field[1, start : start + rows] = pltpu.roll(turned_imag, points, 1) + sign * turned_imag

    half = blocks // 2
    left = lane[:COUNT] < points
    depth = lax.broadcasted_iota(jnp.int32, (SLAB * points, LANES), 0).astype(jnp.bfloat16)
    one, zero = (jnp.full(depth.shape, value, jnp.bfloat16) for value in (1.0, 0.0))
    scale = jnp.exp2(-powers[...])
    last = tiles * COUNT
    for slot in range(out.shape[0]):
        out[slot, last : last + COUNT] = powers[...]

    copies = []
    for k in range(half):
        sources = ([], [])
        for part in range(2):
            for x in range(SLAB):
                lines = []
                for y in range(SLAB):
                    start = (k * SLAB + y) * SLAB + x
                    lines.append(field[part, pl.ds(start, COUNT, stride=rows), :])
                turned = [pltpu.roll(line, points, 1) for line in lines]
                sources[0].append(
                    jnp.concatenate(
                        [jnp.where(left, lines[y], turned[y + 1]) for y in range(0, SLAB, 2)], axis=1
                    )
                )
                sources[1].append(
                    jnp.concatenate(
                        [jnp.where(left, turned[y], lines[y + 1]) for y in range(0, SLAB, 2)], axis=1
                    )
                )
        for side in range(2):
            block = k + half * side
            high, low = halves(jnp.concatenate(sources[side], axis=0))
            match = []
            for j in range(tiles):
                index = grid[pl.ds(block * tiles + j, 1), :] & (SLAB * points - 1)
                index = jnp.broadcast_to(index.astype(jnp.bfloat16), depth.shape)
                match.append(jnp.where(index == depth, one, zero))
            match = jnp.concatenate(match, axis=1)
            values = dot(jnp.concatenate([high, low], axis=0), match)
            count = 2 * SLAB * COUNT
            values = values[:count] + values[count:]
            for j in range(tiles):
                row = block * tiles + j
                at = slice(j * LANES, (j + 1) * LANES)
                total_real = jnp.zeros((COUNT, LANES), jnp.float32)
                total_imag = jnp.zeros((COUNT, LANES), jnp.float32)
                for x in range(SLAB):
                    real = values[x * COUNT : (x + 1) * COUNT, at]
                    imag = values[(SLAB + x) * COUNT : (SLAB + x + 1) * COUNT, at]
                    cosine = waves[2 * x, pl.ds(row, 1), :]
                    sine = waves[2 * x + 1, pl.ds(row, 1), :]
                    total_real += real * cosine + imag * sine
                    total_imag += imag * cosine - real * sine
                total_real *= scale
                total_imag *= scale
                first = jnp.where(left, total_real, pltpu.roll(total_imag, points, 1))
                second = jnp.where(left, pltpu.roll(total_real, points, 1), total_imag)
                out[block, j * COUNT : (j + 1) * COUNT] = first
                out[blocks + block, j * COUNT : (j + 1) * COUNT] = second
            for slot in (block, blocks + block):
                copy = pltpu.make_async_copy(out.at[slot], result.at[slot], sent.at[slot])
                copy.start()
                copies.append(copy)
    for copy in copies:
        copy.wait()


def weight_kernel(scale, partial, coulomb, out):
    half = partial.shape[0] // 2
    last = partial.shape[1] - COUNT
    lane = lax.broadcasted_iota(jnp.int32, (COUNT, LANES), 1)
    own = jnp.where(lane < LANES // 2, 0, 1) == lax.axis_index("tc") // 2
    factors = []
    for j in range(last // COUNT):
        root = jnp.broadcast_to(jnp.sqrt(coulomb[j : j + 1]), (COUNT, LANES))
        factors.append(jnp.where(own, root, pltpu.roll(root, LANES // 2, 1)))
    factor = jnp.concatenate(factors, axis=0)
    pieces = []
    for first in (0, half):
        total = jnp.zeros((last, LANES), jnp.float32)
        for source in range(first, first + half):
            power = jnp.exp2(partial[source, last:])
            total += partial[source, :last] * jnp.concatenate([power] * (last // COUNT), axis=0)
        pieces.append((total * scale) * factor)
    weighted = jnp.concatenate(pieces, axis=0).astype(jnp.bfloat16)
    for target in range(out.shape[0]):
        out[target] = weighted


def panel_kernel(width, gathered, out, terms):
    line, chip = lax.axis_index("tr"), lax.axis_index("tc")
    parity = (chip // 2 + chip + lax.axis_index("ga") // 2) % 2
    senders, height = gathered.shape[0], gathered.shape[1] // 2
    tiles = height // COUNT
    lane = lax.broadcasted_iota(jnp.int32, (1, LANES), 1)
    sign = jnp.where(lane < LANES // 2, -1.0, 1.0).astype(jnp.float32)

    def by_tile(array):
        shape = array.shape[:-2] + (2, tiles, COUNT, LANES)
        array = array.astype(jnp.float32).reshape(shape)
        return [array[..., j, :, :] for j in range(tiles)]

    right = []
    for tile in by_tile(gathered[...]):
        order = [tile[2 * i + low, high] for i in range(senders // 2) for high in range(2) for low in range(2)]
        right.append(jnp.concatenate(order, axis=0).astype(jnp.bfloat16))
    near = by_tile(gathered[2 * line + parity])
    away = by_tile(gathered[2 * line + 1 - parity])
    left = []
    for j in range(tiles):
        order = [(near, away)[far ^ high][j][high] for far in range(2) for high in range(2)]
        tile = jnp.concatenate(order, axis=0)
        turned = pltpu.roll(tile, LANES // 2, 1) * sign
        left.append(jnp.concatenate([tile, turned], axis=0).astype(jnp.bfloat16))
    total = lax.dot_general(
        jnp.concatenate(left, axis=1),
        jnp.concatenate(right, axis=1),
        (((1,), (1,)), ((), ())),
        preferred_element_type=jnp.float32,
    )
    span = terms.shape[2]
    for tile in range(terms.shape[0]):
        terms[tile] = total[:, tile * span : (tile + 1) * span]
    slots = {}
    for far in range(2):
        for side in range(2):
            for column in last_columns(out.shape[0] // 2, far):
                slots[column, 2 * far + side] = len(slots)
    rows = [
        [terms[tile, pl.ds(a, 2 * 4, stride=COUNT), :] for a in range(COUNT)]
        for tile in range(terms.shape[0])
    ]
    for column in range(out.shape[0] // 2):
        tile, start = divmod(column * width, span)
        at = slice(start, start + width)
        line = jnp.concatenate([row[:, at] for row in rows[tile]], axis=1)
        for which in range(4):
            if (column, which) in slots:
                for part in range(2):
                    at = 4 * part + which
                    out[slots[column, which], part : part + 1] = line[at : at + 1]


def sum_kernel(scale, partial, out):
    total = partial[0]
    for source in range(1, partial.shape[0]):
        total += partial[source]
    total *= scale
    width = out.shape[2]
    for row in range(COUNT):
        out[:, row] = total[:, row * width : (row + 1) * width]


def last_columns(groups, far):
    return [g for g in range(groups) if (g // 2) % 2 == far]


def exchange(array, names, groups):
    return lax.all_to_all(
        array, names, split_axis=0, concat_axis=0, tiled=True, axis_index_groups=groups
    )


def body(valence, conduction, envelope, valence_index, conduction_index, grid_index, coulomb):
    points = math.isqrt(valence.shape[-1])
    groups, lines, chips = (lax.axis_size(name) for name in ("ga", "tr", "tc"))
    per_device = coulomb.shape[0]
    tiles = per_device // LANES
    rows = points // 2 * SLAB
    height = tiles * COUNT
    columns = lines * chips * COUNT
    width, span = columns // groups, min(columns, LANES)

    def turned(array):
        lead = array.shape[:-2]
        split = array.reshape(lead + (SLAB, points // 2, LANES))
        return jnp.swapaxes(split, -3, -2).reshape(lead + (rows, LANES))

    smem = pl.BlockSpec(memory_space=pltpu.SMEM)
    vmem = pl.BlockSpec(memory_space=pltpu.VMEM)
    hbm = pl.BlockSpec(memory_space=pl.ANY)
    limit = pltpu.CompilerParams(vmem_limit_bytes=16 * 1024 * 1024)

    by_planes = [
        [(2 * high + low) * groups + g for high in range(2) for g in range(groups)]
        for low in range(2)
    ]
    by_rows = [
        [i * chips + 2 * high + low for i in range(lines) for low in range(2)] for high in range(2)
    ]
    by_columns = [
        [
            (2 * high + (far ^ high ^ parity)) * groups + g
            for far in range(2)
            for high in range(2)
            for g in last_columns(groups, far)
        ]
        for parity in range(2)
    ]

    along_z, along_y, twist = tables(points)
    partial = pl.pallas_call(
        functools.partial(transform_kernel, points),
        out_shape=jax.ShapeDtypeStruct((2 * groups, height + COUNT, LANES), jnp.float32),
        in_specs=[smem] * 2 + [hbm] * 7,
        out_specs=hbm,
        scratch_shapes=[
            pltpu.VMEM((COUNT, 2, rows, LANES), jnp.bfloat16),
            pltpu.VMEM((COUNT, 2, rows, LANES), jnp.bfloat16),
            pltpu.VMEM((2, rows, LANES), jnp.bfloat16),
            pltpu.VMEM((groups * tiles, LANES), jnp.int32),
            pltpu.VMEM(along_z.shape, jnp.float32),
            pltpu.VMEM(along_y.shape, jnp.float32),
            pltpu.VMEM(twist.shape, jnp.float32),
            pltpu.VMEM((2, COUNT * rows, LANES), jnp.float32),
            pltpu.VMEM((2 * SLAB, groups * tiles, LANES), jnp.float32),
            pltpu.VMEM((COUNT, LANES), jnp.float32),
            pltpu.VMEM((2 * groups, height + COUNT, LANES), jnp.float32),
            pltpu.SemaphoreType.DMA((5 + 2 * COUNT,)),
            pltpu.SemaphoreType.DMA((2 * groups,)),
        ],
        compiler_params=pltpu.CompilerParams(vmem_limit_bytes=60 * 1024 * 1024),
        name="transform",
    )(
        valence_index,
        conduction_index,
        turned(valence),
        turned(conduction),
        turned(envelope),
        grid_index.reshape(groups * tiles, LANES),
        along_z,
        along_y,
        twist,
    )
    partial = exchange(partial.astype(jnp.float16), ("tc", "ga"), by_planes).astype(jnp.float32)
    copies = pl.pallas_call(
        functools.partial(weight_kernel, float(points) ** -1.5),
        out_shape=jax.ShapeDtypeStruct((lines * chips // 2, 2 * height, LANES), jnp.bfloat16),
        in_specs=[vmem, vmem],
        out_specs=vmem,
        compiler_params=limit,
        name="weight",
    )(partial, coulomb.reshape(tiles, LANES))
    gathered = exchange(copies, ("tr", "tc"), by_rows)
    terms = pl.pallas_call(
        functools.partial(panel_kernel, width),
        out_shape=jax.ShapeDtypeStruct((2 * groups, 2, COUNT * width), jnp.float32),
        in_specs=[vmem],
        out_specs=vmem,
        scratch_shapes=[pltpu.VMEM((columns // span, 2 * 4 * COUNT, span), jnp.float32)],
        compiler_params=limit,
        name="panel",
    )(gathered)
    terms = exchange(terms, ("tc", "ga"), by_columns)
    return pl.pallas_call(
        functools.partial(sum_kernel, 1.0 / (per_device * groups)),
        out_shape=jax.ShapeDtypeStruct((2, COUNT, width), jnp.float32),
        in_specs=[vmem],
        out_specs=vmem,
        compiler_params=limit,
        name="total",
    )(terms)


def solution(mesh):
    placed = (
        P(None, None, "ga", None),
        P(None, None, "ga", None),
        P(None, "ga", None),
        P(("tr", "tc")),
        P(("tr", "tc")),
        P(),
        P("ga"),
    )
    return jax.shard_map(
        body, mesh=mesh, in_specs=placed, out_specs=P(None, ("tr", "tc"), "ga"), check_vma=False
    )
```

```python
import functools
import math

import jax
import jax.numpy as jnp
import numpy as np
from jax import lax
from jax.experimental import pallas as pl
from jax.experimental.pallas import tpu as pltpu
from jax.sharding import PartitionSpec as P

LANES = 128
COUNT = 8
SLAB = 4


def halves(array):
    high = array.astype(jnp.bfloat16)
    low = (array - high.astype(jnp.float32)).astype(jnp.bfloat16)
    return high, low


def tables(points):
    indices = np.arange(points)
    angles = 2.0 * np.pi * (np.outer(indices, indices) % points) / points
    pair = np.eye(2)
    along_z = np.concatenate([np.kron(pair, np.cos(angles)), np.kron(pair, np.sin(angles))], axis=1)
    half = points // 2
    short = np.arange(half)
    angles = 2.0 * np.pi * (np.outer(short, short) % half) / half
    planes = np.eye(SLAB)
    cosine, sine = np.kron(np.cos(angles), planes), np.kron(np.sin(angles), planes)
    along_y = np.block([[cosine, sine], [-sine, cosine]])
    turn = 2.0 * np.pi * np.repeat(short, SLAB) / points
    ones = np.ones((half * SLAB, points))
    twist = np.stack(
        [
            np.concatenate([ones, ones * np.cos(turn)[:, None]], axis=1),
            np.concatenate([0.0 * ones, ones * -np.sin(turn)[:, None]], axis=1),
        ]
    )

    return tuple(table.astype(np.float32) for table in (along_z, along_y, twist))


def unit_circle(steps, points):
    quarter = points // 4
    shifted = steps + quarter // 2
    turn = (shifted // quarter) & 3
    angle = ((shifted & (quarter - 1)) - quarter // 2).astype(jnp.float32) * (2.0 * math.pi / points)
    square = angle * angle
    sine = angle * (
        1.0 + square * (-1 / 6 + square * (1 / 120 + square * (-1 / 5040 + square * (1 / 362880))))
    )
    cosine = 1.0 + square * (
        -1 / 2
        + square * (1 / 24 + square * (-1 / 720 + square * (1 / 40320 - square * (1 / 3628800))))
    )
    odd = (turn & 1) == 1
    first = jnp.where(odd, sine, cosine)
    second = jnp.where(odd, cosine, sine)
    return (
        jnp.where((turn == 1) | (turn == 2), -first, first),
        jnp.where(turn >= 2, -second, second),
    )


def transform_kernel(
    points,
    valence_ids,
    conduct_ids,
    valence,
    conduction,
    envelope,
    grid_source,
    along_z_source,
    along_y_source,
    twist_source,
    result,
    left_rows,
    right_rows,
    common,
    grid,
    along_z,
    along_y,
    twist,
    field,
    waves,
    powers,
    out,
    arrived,
    sent,
):
    rows = points // 2 * SLAB
    blocks = result.shape[0] // 2
    tiles = grid.shape[0] // blocks
    dot = functools.partial(jnp.dot, preferred_element_type=jnp.float32)

    copies = []

    def fetch(source, target):
        copy = pltpu.make_async_copy(source, target, arrived.at[len(copies)])
        copy.start()
        copies.append(copy)
        return copy

    for source, target in (
        (grid_source, grid),
        (along_z_source, along_z),
        (envelope, common),
        (along_y_source, along_y),
        (twist_source, twist),
    ):
        fetch(source, target)
    for t in range(COUNT):
        fetch(valence.at[:, valence_ids[t]], left_rows.at[t])
        fetch(conduction.at[:, conduct_ids[t]], right_rows.at[t])
    copies[0].wait()

    position = lax.axis_index("ga")
    wave_x = grid[...] // (points * points)
    for plane in range(SLAB):
        steps = ((position * SLAB + plane) * wave_x) & (points - 1)
        cosine, sine = unit_circle(steps, points)
        waves[2 * plane] = cosine
        waves[2 * plane + 1] = sine

    for copy in copies[1:5]:
        copy.wait()

    z_high, z_low = halves(along_z[...])
    z_both = jnp.concatenate([z_high, z_high], axis=0)
    y_high, y_low = halves(along_y[...])

    common_real = common[0].astype(jnp.float32)
    common_imag = common[1].astype(jnp.float32)
    lane = lax.broadcasted_iota(jnp.int32, (rows, LANES), 1)
    sign = jnp.where(lane < points, 1.0, -1.0).astype(jnp.float32)
    for first in range(0, COUNT, 2):
        for copy in copies[5 + 2 * first : 9 + 2 * first]:
            copy.wait()
        parts = []
        for t in (first, first + 1):
            left_real = left_rows[t, 0].astype(jnp.float32)
            left_imag = left_rows[t, 1].astype(jnp.float32)
            right_real = right_rows[t, 0].astype(jnp.float32) + common_real
            right_imag = right_rows[t, 1].astype(jnp.float32) + common_imag
            parts.append(left_real * right_real + left_imag * right_imag)
            parts.append(left_real * right_imag - left_imag * right_real)
            peak = jnp.max(jnp.maximum(jnp.abs(parts[-2]), jnp.abs(parts[-1])), axis=0, keepdims=True)
            peak = jnp.max(peak, axis=1, keepdims=True)
            power = jnp.clip(jnp.ceil(jnp.log2(peak)), -120.0, 120.0)
            powers[t : t + 1] = jnp.broadcast_to(power, (1, LANES))
        high, low = halves(jnp.concatenate(parts, axis=0))
        moved = dot(jnp.concatenate([high, low], axis=1), z_both) + dot(high, z_low)
        columns = []
        for t in range(2):
            real = moved[2 * t * rows : (2 * t + 1) * rows]
            imag = moved[(2 * t + 1) * rows : (2 * t + 2) * rows]
            columns.append(
                jnp.concatenate(
                    [real[:, :LANES] + imag[:, LANES:], imag[:, :LANES] - real[:, LANES:]], axis=0
                )
            )
        high, low = halves(jnp.concatenate(columns, axis=1))
        moved = dot(y_high, high) + (dot(y_high, low) + dot(y_low, high))
        for t in range(2):
            real = moved[:rows, t * LANES : (t + 1) * LANES]
            imag = moved[rows:, t * LANES : (t + 1) * LANES]
            turned_real = real * twist[0] - imag * twist[1]
            turned_imag = real * twist[1] + imag * twist[0]
            start = (first + t) * rows
            field[0, start : start + rows] = pltpu.roll(turned_real, points, 1) + sign * turned_real
            field[1, start : start + rows] = pltpu.roll(turned_imag, points, 1) + sign * turned_imag

    half = blocks // 2
    left = lane[:COUNT] < points
    depth = lax.broadcasted_iota(jnp.int32, (SLAB * points, LANES), 0).astype(jnp.bfloat16)
    one, zero = (jnp.full(depth.shape, value, jnp.bfloat16) for value in (1.0, 0.0))
    scale = jnp.exp2(-powers[...])
    last = tiles * COUNT
    for slot in range(out.shape[0]):
        out[slot, last : last + COUNT] = powers[...]

    copies = []
    for k in range(half):
        sources = ([], [])
        for part in range(2):
            for x in range(SLAB):
                lines = []
                for y in range(SLAB):
                    start = (k * SLAB + y) * SLAB + x
                    lines.append(field[part, pl.ds(start, COUNT, stride=rows), :])
                turned = [pltpu.roll(line, points, 1) for line in lines]
                sources[0].append(
                    jnp.concatenate(
                        [jnp.where(left, lines[y], turned[y + 1]) for y in range(0, SLAB, 2)], axis=1
                    )
                )
                sources[1].append(
                    jnp.concatenate(
                        [jnp.where(left, turned[y], lines[y + 1]) for y in range(0, SLAB, 2)], axis=1
                    )
                )
        for side in range(2):
            block = k + half * side
            high, low = halves(jnp.concatenate(sources[side], axis=0))
            match = []
            for j in range(tiles):
                index = grid[pl.ds(block * tiles + j, 1), :] & (SLAB * points - 1)
                index = jnp.broadcast_to(index.astype(jnp.bfloat16), depth.shape)
                match.append(jnp.where(index == depth, one, zero))
            match = jnp.concatenate(match, axis=1)
            values = dot(jnp.concatenate([high, low], axis=0), match)
            count = 2 * SLAB * COUNT
            values = values[:count] + values[count:]
            for j in range(tiles):
                row = block * tiles + j
                at = slice(j * LANES, (j + 1) * LANES)
                total_real = jnp.zeros((COUNT, LANES), jnp.float32)
                total_imag = jnp.zeros((COUNT, LANES), jnp.float32)
                for x in range(SLAB):
                    real = values[x * COUNT : (x + 1) * COUNT, at]
                    imag = values[(SLAB + x) * COUNT : (SLAB + x + 1) * COUNT, at]
                    cosine = waves[2 * x, pl.ds(row, 1), :]
                    sine = waves[2 * x + 1, pl.ds(row, 1), :]
                    total_real += real * cosine + imag * sine
                    total_imag += imag * cosine - real * sine
                total_real *= scale
                total_imag *= scale
                first = jnp.where(left, total_real, pltpu.roll(total_imag, points, 1))
                second = jnp.where(left, pltpu.roll(total_real, points, 1), total_imag)
                out[block, j * COUNT : (j + 1) * COUNT] = first
                out[blocks + block, j * COUNT : (j + 1) * COUNT] = second
            for slot in (block, blocks + block):
                copy = pltpu.make_async_copy(out.at[slot], result.at[slot], sent.at[slot])
                copy.start()
                copies.append(copy)
    for copy in copies:
        copy.wait()


def weight_kernel(scale, partial, coulomb, out):
    half = partial.shape[0] // 2
    last = partial.shape[1] - COUNT
    lane = lax.broadcasted_iota(jnp.int32, (COUNT, LANES), 1)
    own = jnp.where(lane < LANES // 2, 0, 1) == lax.axis_index("tc") // 2
    factors = []
    for j in range(last // COUNT):
        root = jnp.broadcast_to(jnp.sqrt(coulomb[j : j + 1]), (COUNT, LANES))
        factors.append(jnp.where(own, root, pltpu.roll(root, LANES // 2, 1)))
    factor = jnp.concatenate(factors, axis=0)
    pieces = []
    for first in (0, half):
        total = jnp.zeros((last, LANES), jnp.float32)
        for source in range(first, first + half):
            power = jnp.exp2(partial[source, last:])
            total += partial[source, :last] * jnp.concatenate([power] * (last // COUNT), axis=0)
        pieces.append((total * scale) * factor)
    weighted = jnp.concatenate(pieces, axis=0).astype(jnp.bfloat16)
    for target in range(out.shape[0]):
        out[target] = weighted


def panel_kernel(width, gathered, out, terms):
    line, chip = lax.axis_index("tr"), lax.axis_index("tc")
    parity = (chip // 2 + chip + lax.axis_index("ga") // 2) % 2
    senders, height = gathered.shape[0], gathered.shape[1] // 2
    tiles = height // COUNT
    lane = lax.broadcasted_iota(jnp.int32, (1, LANES), 1)
    sign = jnp.where(lane < LANES // 2, -1.0, 1.0).astype(jnp.float32)

    def by_tile(array):
        shape = array.shape[:-2] + (2, tiles, COUNT, LANES)
        array = array.astype(jnp.float32).reshape(shape)
        return [array[..., j, :, :] for j in range(tiles)]

    right = []
    for tile in by_tile(gathered[...]):
        order = [tile[2 * i + low, high] for i in range(senders // 2) for high in range(2) for low in range(2)]
        right.append(jnp.concatenate(order, axis=0).astype(jnp.bfloat16))
    near = by_tile(gathered[2 * line + parity])
    away = by_tile(gathered[2 * line + 1 - parity])
    left = []
    for j in range(tiles):
        order = [(near, away)[far ^ high][j][high] for far in range(2) for high in range(2)]
        tile = jnp.concatenate(order, axis=0)
        turned = pltpu.roll(tile, LANES // 2, 1) * sign
        left.append(jnp.concatenate([tile, turned], axis=0).astype(jnp.bfloat16))
    total = lax.dot_general(
        jnp.concatenate(left, axis=1),
        jnp.concatenate(right, axis=1),
        (((1,), (1,)), ((), ())),
        preferred_element_type=jnp.float32,
    )
    span = terms.shape[2]
    for tile in range(terms.shape[0]):
        terms[tile] = total[:, tile * span : (tile + 1) * span]
    slots = {}
    for far in range(2):
        for side in range(2):
            for column in last_columns(out.shape[0] // 2, far):
                slots[column, 2 * far + side] = len(slots)
    rows = [
        [terms[tile, pl.ds(a, 2 * 4, stride=COUNT), :] for a in range(COUNT)]
        for tile in range(terms.shape[0])
    ]
    for column in range(out.shape[0] // 2):
        tile, start = divmod(column * width, span)
        at = slice(start, start + width)
        line = jnp.concatenate([row[:, at] for row in rows[tile]], axis=1)
        for which in range(4):
            if (column, which) in slots:
                for part in range(2):
                    at = 4 * part + which
                    out[slots[column, which], part : part + 1] = line[at : at + 1]


def sum_kernel(scale, partial, out):
    total = partial[0]
    for source in range(1, partial.shape[0]):
        total += partial[source]
    total *= scale
    width = out.shape[2]
    for row in range(COUNT):
        out[:, row] = total[:, row * width : (row + 1) * width]


def last_columns(groups, far):
    return [g for g in range(groups) if (g // 2) % 2 == far]


def exchange(array, names, groups):
    return lax.all_to_all(
        array, names, split_axis=0, concat_axis=0, tiled=True, axis_index_groups=groups
    )


def body(valence, conduction, envelope, valence_index, conduction_index, grid_index, coulomb):
    points = math.isqrt(valence.shape[-1])
    groups, lines, chips = (lax.axis_size(name) for name in ("ga", "tr", "tc"))
    per_device = coulomb.shape[0]
    tiles = per_device // LANES
    rows = points // 2 * SLAB
    height = tiles * COUNT
    columns = lines * chips * COUNT
    width, span = columns // groups, min(columns, LANES)

    def turned(array):
        lead = array.shape[:-2]
        split = array.reshape(lead + (SLAB, points // 2, LANES))
        return jnp.swapaxes(split, -3, -2).reshape(lead + (rows, LANES))

    smem = pl.BlockSpec(memory_space=pltpu.SMEM)
    vmem = pl.BlockSpec(memory_space=pltpu.VMEM)
    hbm = pl.BlockSpec(memory_space=pl.ANY)
    limit = pltpu.CompilerParams(vmem_limit_bytes=16 * 1024 * 1024)

    by_planes = [
        [(2 * high + low) * groups + g for high in range(2) for g in range(groups)]
        for low in range(2)
    ]
    by_rows = [
        [i * chips + 2 * high + low for i in range(lines) for low in range(2)] for high in range(2)
    ]
    by_columns = [
        [
            (2 * high + (far ^ high ^ parity)) * groups + g
            for far in range(2)
            for high in range(2)
            for g in last_columns(groups, far)
        ]
        for parity in range(2)
    ]

    along_z, along_y, twist = tables(points)
    partial = pl.pallas_call(
        functools.partial(transform_kernel, points),
        out_shape=jax.ShapeDtypeStruct((2 * groups, height + COUNT, LANES), jnp.float32),
        in_specs=[smem] * 2 + [hbm] * 7,
        out_specs=hbm,
        scratch_shapes=[
            pltpu.VMEM((COUNT, 2, rows, LANES), jnp.bfloat16),
            pltpu.VMEM((COUNT, 2, rows, LANES), jnp.bfloat16),
            pltpu.VMEM((2, rows, LANES), jnp.bfloat16),
            pltpu.VMEM((groups * tiles, LANES), jnp.int32),
            pltpu.VMEM(along_z.shape, jnp.float32),
            pltpu.VMEM(along_y.shape, jnp.float32),
            pltpu.VMEM(twist.shape, jnp.float32),
            pltpu.VMEM((2, COUNT * rows, LANES), jnp.float32),
            pltpu.VMEM((2 * SLAB, groups * tiles, LANES), jnp.float32),
            pltpu.VMEM((COUNT, LANES), jnp.float32),
            pltpu.VMEM((2 * groups, height + COUNT, LANES), jnp.float32),
            pltpu.SemaphoreType.DMA((5 + 2 * COUNT,)),
            pltpu.SemaphoreType.DMA((2 * groups,)),
        ],
        compiler_params=pltpu.CompilerParams(vmem_limit_bytes=60 * 1024 * 1024),
        name="transform",
    )(
        valence_index,
        conduction_index,
        turned(valence),
        turned(conduction),
        turned(envelope),
        grid_index.reshape(groups * tiles, LANES),
        along_z,
        along_y,
        twist,
    )
    partial = exchange(partial.astype(jnp.float16), ("tc", "ga"), by_planes).astype(jnp.float32)
    copies = pl.pallas_call(
        functools.partial(weight_kernel, float(points) ** -1.5),
        out_shape=jax.ShapeDtypeStruct((lines * chips // 2, 2 * height, LANES), jnp.bfloat16),
        in_specs=[vmem, vmem],
        out_specs=vmem,
        compiler_params=limit,
        name="weight",
    )(partial, coulomb.reshape(tiles, LANES))
    gathered = exchange(copies, ("tr", "tc"), by_rows)
    terms = pl.pallas_call(
        functools.partial(panel_kernel, width),
        out_shape=jax.ShapeDtypeStruct((2 * groups, 2, COUNT * width), jnp.float32),
        in_specs=[vmem],
        out_specs=vmem,
        scratch_shapes=[pltpu.VMEM((columns // span, 2 * 4 * COUNT, span), jnp.float32)],
        compiler_params=limit,
        name="panel",
    )(gathered)
    terms = exchange(terms, ("tc", "ga"), by_columns)
    return pl.pallas_call(
        functools.partial(sum_kernel, 1.0 / (per_device * groups)),
        out_shape=jax.ShapeDtypeStruct((2, COUNT, width), jnp.float32),
        in_specs=[vmem],
        out_specs=vmem,
        compiler_params=limit,
        name="total",
    )(terms)


def solution(mesh):
    placed = (
        P(None, None, "ga", None),
        P(None, None, "ga", None),
        P(None, "ga", None),
        P(("tr", "tc")),
        P(("tr", "tc")),
        P(),
        P("ga"),
    )
    return jax.shard_map(
        body, mesh=mesh, in_specs=placed, out_specs=P(None, ("tr", "tc"), "ga"), check_vma=False
    )
```

```python
import functools
import math

import jax
import jax.numpy as jnp
import numpy as np
from jax import lax
from jax.experimental import pallas as pl
from jax.experimental.pallas import tpu as pltpu
from jax.sharding import PartitionSpec as P

LANES = 128
COUNT = 8
SLAB = 4


def halves(array):
    high = array.astype(jnp.bfloat16)
    low = (array - high.astype(jnp.float32)).astype(jnp.bfloat16)
    return high, low


def tables(points):
    indices = np.arange(points)
    angles = 2.0 * np.pi * (np.outer(indices, indices) % points) / points
    pair = np.eye(2)
    along_z = np.concatenate([np.kron(pair, np.cos(angles)), np.kron(pair, np.sin(angles))], axis=1)
    half = points // 2
    short = np.arange(half)
    angles = 2.0 * np.pi * (np.outer(short, short) % half) / half
    planes = np.eye(SLAB)
    cosine, sine = np.kron(np.cos(angles), planes), np.kron(np.sin(angles), planes)
    along_y = np.block([[cosine, sine], [-sine, cosine]])
    turn = 2.0 * np.pi * np.repeat(short, SLAB) / points
    ones = np.ones((half * SLAB, points))
    twist = np.stack(
        [
            np.concatenate([ones, ones * np.cos(turn)[:, None]], axis=1),
            np.concatenate([0.0 * ones, ones * -np.sin(turn)[:, None]], axis=1),
        ]
    )

    return tuple(table.astype(np.float32) for table in (along_z, along_y, twist))


def unit_circle(steps, points):
    quarter = points // 4
    shifted = steps + quarter // 2
    turn = (shifted // quarter) & 3
    angle = ((shifted & (quarter - 1)) - quarter // 2).astype(jnp.float32) * (2.0 * math.pi / points)
    square = angle * angle
    sine = angle * (
        1.0 + square * (-1 / 6 + square * (1 / 120 + square * (-1 / 5040 + square * (1 / 362880))))
    )
    cosine = 1.0 + square * (
        -1 / 2
        + square * (1 / 24 + square * (-1 / 720 + square * (1 / 40320 - square * (1 / 3628800))))
    )
    odd = (turn & 1) == 1
    first = jnp.where(odd, sine, cosine)
    second = jnp.where(odd, cosine, sine)
    return (
        jnp.where((turn == 1) | (turn == 2), -first, first),
        jnp.where(turn >= 2, -second, second),
    )


def transform_kernel(
    points,
    valence_ids,
    conduct_ids,
    valence,
    conduction,
    envelope,
    grid_source,
    along_z_source,
    along_y_source,
    twist_source,
    result,
    left_rows,
    right_rows,
    common,
    grid,
    along_z,
    along_y,
    twist,
    field,
    waves,
    powers,
    out,
    arrived,
    sent,
):
    rows = points // 2 * SLAB
    blocks = result.shape[0] // 2
    tiles = grid.shape[0] // blocks
    dot = functools.partial(jnp.dot, preferred_element_type=jnp.float32)

    copies = []

    def fetch(source, target):
        copy = pltpu.make_async_copy(source, target, arrived.at[len(copies)])
        copy.start()
        copies.append(copy)
        return copy

    for source, target in (
        (grid_source, grid),
        (along_z_source, along_z),
        (envelope, common),
        (along_y_source, along_y),
        (twist_source, twist),
    ):
        fetch(source, target)
    for t in range(COUNT):
        fetch(valence.at[:, valence_ids[t]], left_rows.at[t])
        fetch(conduction.at[:, conduct_ids[t]], right_rows.at[t])
    copies[0].wait()

    position = lax.axis_index("ga")
    wave_x = grid[...] // (points * points)
    for plane in range(SLAB):
        steps = ((position * SLAB + plane) * wave_x) & (points - 1)
        cosine, sine = unit_circle(steps, points)
        waves[2 * plane] = cosine
        waves[2 * plane + 1] = sine

    for copy in copies[1:]:
        copy.wait()

    z_high, z_low = halves(along_z[...])
    z_both = jnp.concatenate([z_high, z_high], axis=0)
    y_high, y_low = halves(along_y[...])

    common_real = common[0].astype(jnp.float32)
    common_imag = common[1].astype(jnp.float32)
    lane = lax.broadcasted_iota(jnp.int32, (rows, LANES), 1)
    sign = jnp.where(lane < points, 1.0, -1.0).astype(jnp.float32)
    for first in range(0, COUNT, 4):
        parts = []
        for t in range(first, first + 4):
            left_real = left_rows[t, 0].astype(jnp.float32)
            left_imag = left_rows[t, 1].astype(jnp.float32)
            right_real = right_rows[t, 0].astype(jnp.float32) + common_real
            right_imag = right_rows[t, 1].astype(jnp.float32) + common_imag
            parts.append(left_real * right_real + left_imag * right_imag)
            parts.append(left_real * right_imag - left_imag * right_real)
            peak = jnp.max(jnp.maximum(jnp.abs(parts[-2]), jnp.abs(parts[-1])), axis=0, keepdims=True)
            peak = jnp.max(peak, axis=1, keepdims=True)
            power = jnp.clip(jnp.ceil(jnp.log2(peak)), -120.0, 120.0)
            powers[t : t + 1] = jnp.broadcast_to(power, (1, LANES))
        high, low = halves(jnp.concatenate(parts, axis=0))
        moved = dot(jnp.concatenate([high, low], axis=1), z_both) + dot(high, z_low)
        columns = []
        for t in range(4):
            real = moved[2 * t * rows : (2 * t + 1) * rows]
            imag = moved[(2 * t + 1) * rows : (2 * t + 2) * rows]
            columns.append(
                jnp.concatenate(
                    [real[:, :LANES] + imag[:, LANES:], imag[:, :LANES] - real[:, LANES:]], axis=0
                )
            )
        high, low = halves(jnp.concatenate(columns, axis=1))
        moved = dot(y_high, high) + (dot(y_high, low) + dot(y_low, high))
        for t in range(4):
            real = moved[:rows, t * LANES : (t + 1) * LANES]
            imag = moved[rows:, t * LANES : (t + 1) * LANES]
            turned_real = real * twist[0] - imag * twist[1]
            turned_imag = real * twist[1] + imag * twist[0]
            start = (first + t) * rows
            field[0, start : start + rows] = pltpu.roll(turned_real, points, 1) + sign * turned_real
            field[1, start : start + rows] = pltpu.roll(turned_imag, points, 1) + sign * turned_imag

    half = blocks // 2
    left = lane[:COUNT] < points
    depth = lax.broadcasted_iota(jnp.int32, (SLAB * points, LANES), 0).astype(jnp.bfloat16)
    one, zero = (jnp.full(depth.shape, value, jnp.bfloat16) for value in (1.0, 0.0))
    scale = jnp.exp2(-powers[...])
    last = tiles * COUNT
    for slot in range(out.shape[0]):
        out[slot, last : last + COUNT] = powers[...]

    copies = []
    for k in range(half):
        sources = ([], [])
        for part in range(2):
            for x in range(SLAB):
                lines = []
                for y in range(SLAB):
                    start = (k * SLAB + y) * SLAB + x
                    lines.append(field[part, pl.ds(start, COUNT, stride=rows), :])
                turned = [pltpu.roll(line, points, 1) for line in lines]
                sources[0].append(
                    jnp.concatenate(
                        [jnp.where(left, lines[y], turned[y + 1]) for y in range(0, SLAB, 2)], axis=1
                    )
                )
                sources[1].append(
                    jnp.concatenate(
                        [jnp.where(left, turned[y], lines[y + 1]) for y in range(0, SLAB, 2)], axis=1
                    )
                )
        for side in range(2):
            block = k + half * side
            high, low = halves(jnp.concatenate(sources[side], axis=0))
            match = []
            for j in range(tiles):
                index = grid[pl.ds(block * tiles + j, 1), :] & (SLAB * points - 1)
                index = jnp.broadcast_to(index.astype(jnp.bfloat16), depth.shape)
                match.append(jnp.where(index == depth, one, zero))
            match = jnp.concatenate(match, axis=1)
            values = dot(jnp.concatenate([high, low], axis=0), match)
            count = 2 * SLAB * COUNT
            values = values[:count] + values[count:]
            for j in range(tiles):
                row = block * tiles + j
                at = slice(j * LANES, (j + 1) * LANES)
                total_real = jnp.zeros((COUNT, LANES), jnp.float32)
                total_imag = jnp.zeros((COUNT, LANES), jnp.float32)
                for x in range(SLAB):
                    real = values[x * COUNT : (x + 1) * COUNT, at]
                    imag = values[(SLAB + x) * COUNT : (SLAB + x + 1) * COUNT, at]
                    cosine = waves[2 * x, pl.ds(row, 1), :]
                    sine = waves[2 * x + 1, pl.ds(row, 1), :]
                    total_real += real * cosine + imag * sine
                    total_imag += imag * cosine - real * sine
                total_real *= scale
                total_imag *= scale
                first = jnp.where(left, total_real, pltpu.roll(total_imag, points, 1))
                second = jnp.where(left, pltpu.roll(total_real, points, 1), total_imag)
                out[block, j * COUNT : (j + 1) * COUNT] = first
                out[blocks + block, j * COUNT : (j + 1) * COUNT] = second
            for slot in (block, blocks + block):
                copy = pltpu.make_async_copy(out.at[slot], result.at[slot], sent.at[slot])
                copy.start()
                copies.append(copy)
    for copy in copies:
        copy.wait()


def weight_kernel(scale, partial, coulomb, out):
    half = partial.shape[0] // 2
    last = partial.shape[1] - COUNT
    lane = lax.broadcasted_iota(jnp.int32, (COUNT, LANES), 1)
    own = jnp.where(lane < LANES // 2, 0, 1) == lax.axis_index("tc") // 2
    factors = []
    for j in range(last // COUNT):
        root = jnp.broadcast_to(jnp.sqrt(coulomb[j : j + 1]), (COUNT, LANES))
        factors.append(jnp.where(own, root, pltpu.roll(root, LANES // 2, 1)))
    factor = jnp.concatenate(factors, axis=0)
    pieces = []
    for first in (0, half):
        total = jnp.zeros((last, LANES), jnp.float32)
        for source in range(first, first + half):
            power = jnp.exp2(partial[source, last:])
            total += partial[source, :last] * jnp.concatenate([power] * (last // COUNT), axis=0)
        pieces.append((total * scale) * factor)
    weighted = jnp.concatenate(pieces, axis=0).astype(jnp.bfloat16)
    for target in range(out.shape[0]):
        out[target] = weighted


def panel_kernel(width, gathered, out, terms):
    line, chip = lax.axis_index("tr"), lax.axis_index("tc")
    parity = (chip // 2 + chip + lax.axis_index("ga") // 2) % 2
    senders, height = gathered.shape[0], gathered.shape[1] // 2
    tiles = height // COUNT
    lane = lax.broadcasted_iota(jnp.int32, (1, LANES), 1)
    sign = jnp.where(lane < LANES // 2, -1.0, 1.0).astype(jnp.float32)

    def by_tile(array):
        shape = array.shape[:-2] + (2, tiles, COUNT, LANES)
        array = array.astype(jnp.float32).reshape(shape)
        return [array[..., j, :, :] for j in range(tiles)]

    right = []
    for tile in by_tile(gathered[...]):
        order = [tile[2 * i + low, high] for i in range(senders // 2) for high in range(2) for low in range(2)]
        right.append(jnp.concatenate(order, axis=0).astype(jnp.bfloat16))
    near = by_tile(gathered[2 * line + parity])
    away = by_tile(gathered[2 * line + 1 - parity])
    left = []
    for j in range(tiles):
        order = [(near, away)[far ^ high][j][high] for far in range(2) for high in range(2)]
        tile = jnp.concatenate(order, axis=0)
        turned = pltpu.roll(tile, LANES // 2, 1) * sign
        left.append(jnp.concatenate([tile, turned], axis=0).astype(jnp.bfloat16))
    total = lax.dot_general(
        jnp.concatenate(left, axis=1),
        jnp.concatenate(right, axis=1),
        (((1,), (1,)), ((), ())),
        preferred_element_type=jnp.float32,
    )
    span = terms.shape[2]
    for tile in range(terms.shape[0]):
        terms[tile] = total[:, tile * span : (tile + 1) * span]
    slots = {}
    for far in range(2):
        for side in range(2):
            for column in last_columns(out.shape[0] // 2, far):
                slots[column, 2 * far + side] = len(slots)
    rows = [
        [terms[tile, pl.ds(a, 2 * 4, stride=COUNT), :] for a in range(COUNT)]
        for tile in range(terms.shape[0])
    ]
    for column in range(out.shape[0] // 2):
        tile, start = divmod(column * width, span)
        at = slice(start, start + width)
        line = jnp.concatenate([row[:, at] for row in rows[tile]], axis=1)
        for which in range(4):
            if (column, which) in slots:
                for part in range(2):
                    at = 4 * part + which
                    out[slots[column, which], part : part + 1] = line[at : at + 1]


def sum_kernel(scale, partial, out):
    total = partial[0]
    for source in range(1, partial.shape[0]):
        total += partial[source]
    total *= scale
    width = out.shape[2]
    for row in range(COUNT):
        out[:, row] = total[:, row * width : (row + 1) * width]


def last_columns(groups, far):
    return [g for g in range(groups) if (g // 2) % 2 == far]


def exchange(array, names, groups):
    return lax.all_to_all(
        array, names, split_axis=0, concat_axis=0, tiled=True, axis_index_groups=groups
    )


def body(valence, conduction, envelope, valence_index, conduction_index, grid_index, coulomb):
    points = math.isqrt(valence.shape[-1])
    groups, lines, chips = (lax.axis_size(name) for name in ("ga", "tr", "tc"))
    per_device = coulomb.shape[0]
    tiles = per_device // LANES
    rows = points // 2 * SLAB
    height = tiles * COUNT
    columns = lines * chips * COUNT
    width, span = columns // groups, min(columns, LANES)

    def turned(array):
        lead = array.shape[:-2]
        split = array.reshape(lead + (SLAB, points // 2, LANES))
        return jnp.swapaxes(split, -3, -2).reshape(lead + (rows, LANES))

    smem = pl.BlockSpec(memory_space=pltpu.SMEM)
    vmem = pl.BlockSpec(memory_space=pltpu.VMEM)
    hbm = pl.BlockSpec(memory_space=pl.ANY)
    limit = pltpu.CompilerParams(vmem_limit_bytes=16 * 1024 * 1024)

    by_planes = [
        [(2 * high + low) * groups + g for high in range(2) for g in range(groups)]
        for low in range(2)
    ]
    by_rows = [
        [i * chips + 2 * high + low for i in range(lines) for low in range(2)] for high in range(2)
    ]
    by_columns = [
        [
            (2 * high + (far ^ high ^ parity)) * groups + g
            for far in range(2)
            for high in range(2)
            for g in last_columns(groups, far)
        ]
        for parity in range(2)
    ]

    along_z, along_y, twist = tables(points)
    partial = pl.pallas_call(
        functools.partial(transform_kernel, points),
        out_shape=jax.ShapeDtypeStruct((2 * groups, height + COUNT, LANES), jnp.float32),
        in_specs=[smem] * 2 + [hbm] * 7,
        out_specs=hbm,
        scratch_shapes=[
            pltpu.VMEM((COUNT, 2, rows, LANES), jnp.bfloat16),
            pltpu.VMEM((COUNT, 2, rows, LANES), jnp.bfloat16),
            pltpu.VMEM((2, rows, LANES), jnp.bfloat16),
            pltpu.VMEM((groups * tiles, LANES), jnp.int32),
            pltpu.VMEM(along_z.shape, jnp.float32),
            pltpu.VMEM(along_y.shape, jnp.float32),
            pltpu.VMEM(twist.shape, jnp.float32),
            pltpu.VMEM((2, COUNT * rows, LANES), jnp.float32),
            pltpu.VMEM((2 * SLAB, groups * tiles, LANES), jnp.float32),
            pltpu.VMEM((COUNT, LANES), jnp.float32),
            pltpu.VMEM((2 * groups, height + COUNT, LANES), jnp.float32),
            pltpu.SemaphoreType.DMA((5 + 2 * COUNT,)),
            pltpu.SemaphoreType.DMA((2 * groups,)),
        ],
        compiler_params=pltpu.CompilerParams(vmem_limit_bytes=60 * 1024 * 1024),
        name="transform",
    )(
        valence_index,
        conduction_index,
        turned(valence),
        turned(conduction),
        turned(envelope),
        grid_index.reshape(groups * tiles, LANES),
        along_z,
        along_y,
        twist,
    )
    partial = exchange(partial.astype(jnp.float16), ("tc", "ga"), by_planes).astype(jnp.float32)
    copies = pl.pallas_call(
        functools.partial(weight_kernel, float(points) ** -1.5),
        out_shape=jax.ShapeDtypeStruct((lines * chips // 2, 2 * height, LANES), jnp.bfloat16),
        in_specs=[vmem, vmem],
        out_specs=vmem,
        compiler_params=limit,
        name="weight",
    )(partial, coulomb.reshape(tiles, LANES))
    gathered = exchange(copies, ("tr", "tc"), by_rows)
    terms = pl.pallas_call(
        functools.partial(panel_kernel, width),
        out_shape=jax.ShapeDtypeStruct((2 * groups, 2, COUNT * width), jnp.float32),
        in_specs=[vmem],
        out_specs=vmem,
        scratch_shapes=[pltpu.VMEM((columns // span, 2 * 4 * COUNT, span), jnp.float32)],
        compiler_params=limit,
        name="panel",
    )(gathered)
    terms = exchange(terms, ("tc", "ga"), by_columns)
    return pl.pallas_call(
        functools.partial(sum_kernel, 1.0 / (per_device * groups)),
        out_shape=jax.ShapeDtypeStruct((2, COUNT, width), jnp.float32),
        in_specs=[vmem],
        out_specs=vmem,
        compiler_params=limit,
        name="total",
    )(terms)


def solution(mesh):
    placed = (
        P(None, None, "ga", None),
        P(None, None, "ga", None),
        P(None, "ga", None),
        P(("tr", "tc")),
        P(("tr", "tc")),
        P(),
        P("ga"),
    )
    return jax.shard_map(
        body, mesh=mesh, in_specs=placed, out_specs=P(None, ("tr", "tc"), "ga"), check_vma=False
    )
```
